512 devices in a mesh: feat: 128 (over x_hi, z, y), tok: 4 (over x_lo, core).
Axes of the slice: x: 4 (x_hi: 2, x_lo: 2; x = x_hi * 2 + x_lo), y: 4, z: 16, core: 2. Of those that a mesh axis runs over, the one named last changes fastest.
Arguments:
- layer_inputs: bfloat16 [3, 256, 4096], P(None, 'feat', 'tok'), may hold values from -6 to 6
- targets: bfloat16 [3, 256, 4096], P(None, 'feat', 'tok'), may hold values from -6 to 6
- winners: int32 [3, 256, 64], replicated, may hold values from 0 to 16383, all different within a row
- encoder_weight: bfloat16 [3, 4096, 16384], P(None, 'tok', 'feat'), may hold values from -0.09375 to 0.09375
- encoder_bias: float32 [3, 16384], P(None, 'feat'), may hold values from -3 to 3
- decoder_weight: bfloat16 [6, 16384, 4096], P(None, 'feat', 'tok'), may hold values from -0.75 to 0.75
- decoder_bias: float32 [3, 4096], P(None, 'tok'), may hold values from -3 to 3
Outputs:
- recon: bfloat16 [3, 256, 4096], P(None, 'feat', 'tok')
- encoder_grad: bfloat16 [3, 4096, 16384], P(None, 'tok', 'feat')
- encoder_bias_grad: float32 [3, 16384], P(None, 'feat')
- decoder_grad: bfloat16 [6, 16384, 4096], P(None, 'feat', 'tok')
- decoder_bias_grad: float32 [3, 4096], P(None, 'tok')
The draws below stay inside these ranges and needn't reach their ends.
Inputs may be any that keep to these rules, and one draw needn't show every extreme that they name: For each layer and token the 64 winners are distinct; every feature number is a winner somewhere.
All inputs are finite; a program needn't handle non-finite values.
Results may differ from the reference program's by a relative error of at most 0.0062.
Values may be sent and summed in bfloat16 or wider, within the bound.
No kernel may reach another device: no remote copies, remote signals or barrier semaphores. Data moves between devices by JAX's collectives and lax.ppermute only.
A program may use at most 64 MiB of HBM per device.

```python
import jax
import jax.numpy as jnp
from jax import lax

D = 4096
F = 16384
K = 64
L = 3
PAIRS = 6
TOKENS = 256


def block_levels(own_key, shape, cuts, smallest, largest):
    factor_of, own = 1.0, jax.random.fold_in(own_key, 6)
    for dim, blocks in cuts:
        heights = jnp.exp(jax.random.uniform(jax.random.fold_in(own, dim), (blocks,), jnp.float32, smallest / len(cuts), largest / len(cuts)))
        factor_of = factor_of * jnp.repeat(heights, shape[dim] // blocks).reshape([-1 if axis == dim else 1 for axis in range(len(shape))])
    return factor_of


def choose_distinct(own_key, rows, count, top, lift):
    order = jax.random.permutation(jax.random.fold_in(own_key, 1), count)
    boost = order
    for power in range(3):
        boost = boost * boost // count
    boost = boost * lift // count
    chance = jax.random.randint(jax.random.fold_in(own_key, 2), (rows, count), 0, 4096) + boost
    holders = jax.random.permutation(jax.random.fold_in(own_key, 3), rows)[jnp.arange(count) % rows]
    chance = jnp.where(jnp.arange(rows)[:, None] == holders[None, :], 1 << 14, chance)
    priority = chance * count + jnp.arange(count)
    return lax.top_k(priority.astype(jnp.int32), top)[1].astype(jnp.int32)


def normal_values(stream_key, shape, spread, limit, cuts=(), kind=jnp.bfloat16):
    values = spread * jax.random.normal(stream_key, shape, jnp.float32)
    if cuts:
        values = values * block_levels(stream_key, shape, cuts, -0.22, 0.18)
    return jnp.clip(values, -limit, limit).astype(kind)


def setup_inputs(seed: int = 0) -> dict:
    arg_keys = jax.random.split(jax.random.key(seed), 8)
    return {
        "layer_inputs": normal_values(arg_keys[0], (L, TOKENS, D), 1.0, 6.0, ((1, 128), (2, 4))),
        "targets": normal_values(arg_keys[1], (L, TOKENS, D), 1.0, 6.0, ((1, 128), (2, 4))),
        "winners": choose_distinct(arg_keys[2], L * TOKENS, F, K, 64).reshape((L, TOKENS, K)),
        "encoder_weight": normal_values(arg_keys[3], (L, D, F), D ** -0.5, 0.09375, ((1, 4), (2, 128))),
        "encoder_bias": normal_values(arg_keys[4], (L, F), 0.5, 3.0, ((1, 128),), jnp.float32),
        "decoder_weight": normal_values(arg_keys[5], (PAIRS, F, D), K ** -0.5, 0.75, ((1, 128), (2, 4))),
        "decoder_bias": normal_values(arg_keys[6], (L, D), 0.5, 3.0, ((1, 4),), jnp.float32),
    }


def pair_number(source, target_layer):
    return sum(L - before for before in range(source)) + target_layer - source


def reference(layer_inputs, targets, winners, encoder_weight, encoder_bias, decoder_weight, decoder_bias):
    activation = []
    chosen_all = []
    token_ids = jnp.arange(TOKENS, dtype=jnp.int32)[:, None]
    for layer in range(L):
        pre_acts = jnp.dot(layer_inputs[layer], encoder_weight[layer], preferred_element_type=jnp.float32) + encoder_bias[layer]
        chosen = jnp.zeros((TOKENS, F), jnp.float32).at[token_ids, winners[layer]].set(1.0) > 0.5
        chosen_all.append(chosen)
        activation.append(jnp.where(chosen, pre_acts, 0.0).astype(jnp.bfloat16))
    recon_list = []
    error_list = []
    for target_layer in range(L):
        totals = jnp.zeros((TOKENS, D), jnp.float32)
        for source in range(target_layer + 1):
            totals = totals + jnp.dot(activation[source], decoder_weight[pair_number(source, target_layer)], preferred_element_type=jnp.float32)
        totals = totals + decoder_bias[target_layer]
        recon_list.append(totals.astype(jnp.bfloat16))
        error_list.append((totals - targets[target_layer].astype(jnp.float32)).astype(jnp.bfloat16))
    encoder_grads = []
    encoder_bias_grads = []
    decoder_grads = [None] * PAIRS
    for source in range(L):
        grad_act = jnp.zeros((TOKENS, F), jnp.float32)
        for target_layer in range(source, L):
            pair_slot = pair_number(source, target_layer)
            grad_act = grad_act + jnp.dot(error_list[target_layer], decoder_weight[pair_slot].T, preferred_element_type=jnp.float32)
            decoder_grads[pair_slot] = jnp.dot(activation[source].T, error_list[target_layer], preferred_element_type=jnp.float32).astype(jnp.bfloat16)
        grad_pre = jnp.where(chosen_all[source], grad_act, 0.0).astype(jnp.bfloat16)
        encoder_grads.append(jnp.dot(layer_inputs[source].T, grad_pre, preferred_element_type=jnp.float32).astype(jnp.bfloat16))
        encoder_bias_grads.append(jnp.sum(grad_pre.astype(jnp.float32), axis=0))
    decoder_bias_grads = [jnp.sum(error_list[layer].astype(jnp.float32), axis=0) for layer in range(L)]
    return (jnp.stack(recon_list), jnp.stack(encoder_grads), jnp.stack(encoder_bias_grads), jnp.stack(decoder_grads), jnp.stack(decoder_bias_grads))
```

```python
import jax
import jax.numpy as jnp
from jax import lax
from jax.sharding import Mesh, PartitionSpec as P

FEAT = ("xh", "z", "y")
TOK = ("xl", "core")
PLANE = ("xh", "y")
XH, Z, Y, XL, CORE = 2, 16, 4, 2, 2
bf16, f32 = jnp.bfloat16, jnp.float32


def pair_number(source, target_layer, layers):
    return sum((layers - before for before in range(source))) + target_layer - source


def swap(x, axis):
    return lax.ppermute(x, axis, [(0, 1), (1, 0)])


def gather_tokens(home):
    layers, rows, width = home.shape
    along_z = lax.all_to_all(
        jnp.broadcast_to(home[None], (Z, layers, rows, width)), "z", 0, 0
    )
    block = along_z.transpose(1, 0, 2, 3).reshape(1, layers, Z * rows, width)
    return lax.all_to_all(
        jnp.broadcast_to(block, (XH * Y,) + block.shape[1:]), PLANE, 0, 0
    )


def scatter_tokens(partial):
    planes, layers, rows, width = partial.shape
    got = lax.all_to_all(partial.astype(bf16), PLANE, 0, 0)
    summed = jnp.sum(got.astype(f32), axis=0).astype(bf16)
    blocks = summed.reshape(layers, Z, rows // Z, width).transpose(1, 0, 2, 3)
    got = lax.all_to_all(blocks, "z", 0, 0)
    return jnp.sum(got.astype(f32), axis=0)


def sum_tok(partial):
    both = partial + swap(partial, "core")
    mine = both.astype(bf16)
    return mine.astype(f32) + swap(mine, "xl").astype(f32)


def body(
    layer_inputs, targets, winners, encoder_weight, encoder_bias, decoder_weight, decoder_bias
):
    layers = layer_inputs.shape[0]
    width_here = encoder_weight.shape[2]
    picks = winners.shape[2]
    tokens = winners.shape[1]
    model = encoder_weight.shape[1]

    gathered = gather_tokens(layer_inputs)
    x = [gathered[:, l].reshape(tokens, model) for l in range(layers)]

    order = winners.reshape(layers, XH, Z, Y, 2, picks).transpose(0, 1, 3, 2, 4, 5)
    order = order.reshape(layers, tokens, picks)
    feature_ids = lax.axis_index(FEAT) * width_here + jnp.arange(width_here, dtype=jnp.int32)
    chosen = jnp.zeros((layers, tokens, width_here), jnp.bool_)
    for offset in range(0, picks, 8):
        matches = order[:, :, offset : offset + 8, None] == feature_ids
        chosen = jnp.logical_or(chosen, jnp.any(matches, axis=2))

    partial_pre = jnp.stack(
        [jnp.dot(x[l], encoder_weight[l], preferred_element_type=f32) for l in range(layers)]
    )
    pre_acts = sum_tok(partial_pre) + encoder_bias[:, None, :]
    activation = jnp.where(chosen, pre_acts, 0.0).astype(bf16)
    decoded = []
    for target_layer in range(layers):
        partial_sum = None
        for source in range(target_layer + 1):
            product = jnp.dot(
                activation[source],
                decoder_weight[pair_number(source, target_layer, layers)],
                preferred_element_type=f32,
            )
            partial_sum = product if partial_sum is None else partial_sum + product
        decoded.append(partial_sum.astype(bf16).reshape(XH * Y, tokens // (XH * Y), model))
    summed = scatter_tokens(jnp.stack(decoded, axis=1)) + decoder_bias[:, None, :]
    recon = summed.astype(bf16)
    errors_home = (summed - targets.astype(f32)).astype(bf16)
    errors_got = gather_tokens(errors_home)
    errors_all = [errors_got[:, l].reshape(tokens, model) for l in range(layers)]
    partial_grad = []
    decoder_grads = [None] * decoder_weight.shape[0]
    for source in range(layers):
        grad_act = None
        for target_layer in range(source, layers):
            pair_slot = pair_number(source, target_layer, layers)
            product = lax.dot_general(
                errors_all[target_layer],
                decoder_weight[pair_slot],
                (((1,), (1,)), ((), ())),
                preferred_element_type=f32,
            )
            grad_act = product if grad_act is None else grad_act + product
            decoder_grads[pair_slot] = lax.dot_general(
                activation[source],
                errors_all[target_layer],
                (((0,), (0,)), ((), ())),
                preferred_element_type=f32,
            ).astype(bf16)
        partial_grad.append(grad_act)
    grad_act_all = sum_tok(jnp.stack(partial_grad))
    grad_pre = jnp.where(chosen, grad_act_all, 0.0).astype(bf16)
    encoder_grad = jnp.stack(
        [
            lax.dot_general(
                x[l], grad_pre[l], (((0,), (0,)), ((), ())), preferred_element_type=f32
            ).astype(bf16)
            for l in range(layers)
        ]
    )
    encoder_bias_grad = jnp.sum(grad_pre.astype(f32), axis=1)
    decoder_bias_grad = jnp.sum(errors_got.astype(f32), axis=(0, 2))
    return (recon, encoder_grad, encoder_bias_grad, jnp.stack(decoder_grads), decoder_bias_grad)


def solution(mesh):
    fine = Mesh(mesh.devices.reshape(XH, Z, Y, XL, CORE), FEAT + TOK)
    in_specs = (
        P(None, FEAT, TOK),
        P(None, FEAT, TOK),
        P(),
        P(None, TOK, FEAT),
        P(None, FEAT),
        P(None, FEAT, TOK),
        P(None, TOK),
    )
    out_specs = (
        P(None, FEAT, TOK),
        P(None, TOK, FEAT),
        P(None, FEAT),
        P(None, FEAT, TOK),
        P(None, TOK),
    )
    return jax.shard_map(body, mesh=fine, in_specs=in_specs, out_specs=out_specs, check_vma=False)
```

```python
import jax
import jax.numpy as jnp
from jax import lax
from jax.sharding import Mesh, PartitionSpec as P

FEAT = ("xh", "z", "y")
TOK = ("xl", "core")
PLANE = ("xh", "y")
XH, Z, Y, XL, CORE = 2, 16, 4, 2, 2
bf16, f32 = jnp.bfloat16, jnp.float32


def pair_number(source, target_layer, layers):
    return sum((layers - before for before in range(source))) + target_layer - source


def swap(x, axis):
    return lax.ppermute(x, axis, [(0, 1), (1, 0)])


def gather_z(home):
    layers, rows, width = home.shape
    return lax.all_to_all(jnp.broadcast_to(home[None], (Z, layers, rows, width)), "z", 0, 0)


def gather_plane(along_z):
    _, layers, rows, width = along_z.shape
    block = along_z.transpose(1, 0, 2, 3).reshape(1, layers, Z * rows, width)
    return lax.all_to_all(
        jnp.broadcast_to(block, (XH * Y,) + block.shape[1:]), PLANE, 0, 0
    )


def scatter_tokens(partial):
    planes, layers, rows, width = partial.shape
    got = lax.all_to_all(partial.astype(bf16), PLANE, 0, 0)
    summed = jnp.sum(got.astype(f32), axis=0).astype(bf16)
    blocks = summed.reshape(layers, Z, rows // Z, width).transpose(1, 0, 2, 3)
    got = lax.all_to_all(blocks, "z", 0, 0)
    return jnp.sum(got.astype(f32), axis=0)


def sum_tok(partial):
    both = partial + swap(partial, "core")
    mine = both.astype(bf16)
    return mine.astype(f32) + swap(mine, "xl").astype(f32)


def body(
    layer_inputs, targets, winners, encoder_weight, encoder_bias, decoder_weight, decoder_bias
):
    layers = layer_inputs.shape[0]
    width_here = encoder_weight.shape[2]
    picks = winners.shape[2]
    tokens = winners.shape[1]
    model = encoder_weight.shape[1]

    along_z, winners = lax.optimization_barrier((gather_z(layer_inputs), winners))
    gathered = gather_plane(along_z)
    x = [gathered[:, l].reshape(tokens, model) for l in range(layers)]

    order = winners.reshape(layers, XH, Z, Y, 2, picks).transpose(0, 1, 3, 2, 4, 5)
    order = order.reshape(layers, tokens, picks)
    feature_ids = lax.axis_index(FEAT) * width_here + jnp.arange(width_here, dtype=jnp.int32)
    chosen = jnp.zeros((layers, tokens, width_here), jnp.bool_)
    for offset in range(0, picks, 8):
        matches = order[:, :, offset : offset + 8, None] == feature_ids
        chosen = jnp.logical_or(chosen, jnp.any(matches, axis=2))

    partial_pre = jnp.stack(
        [jnp.dot(x[l], encoder_weight[l], preferred_element_type=f32) for l in range(layers)]
    )
    partial_pre, chosen = lax.optimization_barrier((partial_pre, chosen))
    pre_acts = sum_tok(partial_pre) + encoder_bias[:, None, :]
    activation = jnp.where(chosen, pre_acts, 0.0).astype(bf16)
    decoded = []
    for target_layer in range(layers):
        partial_sum = None
        for source in range(target_layer + 1):
            product = jnp.dot(
                activation[source],
                decoder_weight[pair_number(source, target_layer, layers)],
                preferred_element_type=f32,
            )
            partial_sum = product if partial_sum is None else partial_sum + product
        decoded.append(partial_sum.astype(bf16).reshape(XH * Y, tokens // (XH * Y), model))
    summed = scatter_tokens(jnp.stack(decoded, axis=1)) + decoder_bias[:, None, :]
    recon = summed.astype(bf16)
    errors_home = (summed - targets.astype(f32)).astype(bf16)
    errors_got = gather_plane(gather_z(errors_home))
    errors_all = [errors_got[:, l].reshape(tokens, model) for l in range(layers)]
    partial_grad = []
    for source in range(layers):
        grad_act = None
        for target_layer in range(source, layers):
            product = lax.dot_general(
                errors_all[target_layer],
                decoder_weight[pair_number(source, target_layer, layers)],
                (((1,), (1,)), ((), ())),
                preferred_element_type=f32,
            )
            grad_act = product if grad_act is None else grad_act + product
        partial_grad.append(grad_act)
    partial_grad = jnp.stack(partial_grad)
    both, errors_got = lax.optimization_barrier((swap(partial_grad, "core"), errors_got))
    both = (partial_grad + both).astype(bf16)
    errors_all = [errors_got[:, l].reshape(tokens, model) for l in range(layers)]
    decoder_grads = [
        lax.dot_general(
            activation[source],
            errors_all[target_layer],
            (((0,), (0,)), ((), ())),
            preferred_element_type=f32,
        ).astype(bf16)
        for source in range(layers)
        for target_layer in range(source, layers)
    ]
    grad_act_all = both.astype(f32) + swap(both, "xl").astype(f32)
    grad_pre = jnp.where(chosen, grad_act_all, 0.0).astype(bf16)
    encoder_grad = jnp.stack(
        [
            lax.dot_general(
                x[l], grad_pre[l], (((0,), (0,)), ((), ())), preferred_element_type=f32
            ).astype(bf16)
            for l in range(layers)
        ]
    )
    encoder_bias_grad = jnp.sum(grad_pre.astype(f32), axis=1)
    decoder_bias_grad = jnp.sum(errors_got.astype(f32), axis=(0, 2))
    return (recon, encoder_grad, encoder_bias_grad, jnp.stack(decoder_grads), decoder_bias_grad)


def solution(mesh):
    fine = Mesh(mesh.devices.reshape(XH, Z, Y, XL, CORE), FEAT + TOK)
    in_specs = (
        P(None, FEAT, TOK),
        P(None, FEAT, TOK),
        P(),
        P(None, TOK, FEAT),
        P(None, FEAT),
        P(None, FEAT, TOK),
        P(None, TOK),
    )
    out_specs = (
        P(None, FEAT, TOK),
        P(None, TOK, FEAT),
        P(None, FEAT),
        P(None, FEAT, TOK),
        P(None, TOK),
    )
    return jax.shard_map(body, mesh=fine, in_specs=in_specs, out_specs=out_specs, check_vma=False)
```

```python
import jax
import jax.numpy as jnp
from jax import lax
from jax.sharding import Mesh, PartitionSpec as P

FEAT = ("xh", "z", "y")
TOK = ("xl", "core")
PLANE = ("xh", "y")
XH, Z, Y, XL, CORE = 2, 16, 4, 2, 2
bf16, f32 = jnp.bfloat16, jnp.float32


def pair_number(source, target_layer, layers):
    return sum((layers - before for before in range(source))) + target_layer - source


def swap(x, axis):
    return lax.ppermute(x, axis, [(0, 1), (1, 0)])


def gather_z(home):
    layers, rows, width = home.shape
    return lax.all_to_all(jnp.broadcast_to(home[None], (Z, layers, rows, width)), "z", 0, 0)


def gather_plane(along_z):
    _, layers, rows, width = along_z.shape
    block = along_z.transpose(1, 0, 2, 3).reshape(1, layers, Z * rows, width)
    return lax.all_to_all(
        jnp.broadcast_to(block, (XH * Y,) + block.shape[1:]), PLANE, 0, 0
    )


def scatter_plane(partial):
    got = lax.all_to_all(partial, PLANE, 0, 0)
    return jnp.sum(got.astype(f32), axis=0).astype(bf16)


def scatter_z(summed):
    layers, rows, width = summed.shape
    blocks = summed.reshape(layers, Z, rows // Z, width).transpose(1, 0, 2, 3)
    got = lax.all_to_all(blocks, "z", 0, 0)
    return jnp.sum(got.astype(f32), axis=0)


def sum_tok(partial):
    both = partial + swap(partial, "core")
    mine = both.astype(bf16)
    return mine.astype(f32) + swap(mine, "xl").astype(f32)


def body(
    layer_inputs, targets, winners, encoder_weight, encoder_bias, decoder_weight, decoder_bias
):
    layers = layer_inputs.shape[0]
    width_here = encoder_weight.shape[2]
    picks = winners.shape[2]
    tokens = winners.shape[1]
    model = encoder_weight.shape[1]

    early = layers - 1
    along_z = gather_z(layer_inputs)
    gathered = [gather_plane(along_z[:, :early]), gather_plane(along_z[:, early:])]
    x = [
        g[:, l].reshape(tokens, model) for g in gathered for l in range(g.shape[1])
    ]

    order = winners.reshape(layers, XH, Z, Y, 2, picks).transpose(0, 1, 3, 2, 4, 5)
    order = order.reshape(layers, tokens, picks)
    feature_ids = lax.axis_index(FEAT) * width_here + jnp.arange(width_here, dtype=jnp.int32)
    chosen = jnp.zeros((layers, tokens, width_here), jnp.bool_)
    for offset in range(0, picks, 8):
        matches = order[:, :, offset : offset + 8, None] == feature_ids
        chosen = jnp.logical_or(chosen, jnp.any(matches, axis=2))

    def encode(first, last):
        return jnp.stack(
            [
                jnp.dot(x[l], encoder_weight[l], preferred_element_type=f32)
                for l in range(first, last)
            ]
        )

    def act(pre_acts, first, last):
        pre_acts = pre_acts + encoder_bias[first:last, None, :]
        return jnp.where(chosen[first:last], pre_acts, 0.0).astype(bf16)

    def decode(target_layer, sources):
        partial_sum = None
        for source in sources:
            product = jnp.dot(
                activation[source],
                decoder_weight[pair_number(source, target_layer, layers)],
                preferred_element_type=f32,
            )
            partial_sum = product if partial_sum is None else partial_sum + product
        return partial_sum

    def by_plane(totals):
        return jnp.stack(
            [t.astype(bf16).reshape(XH * Y, tokens // (XH * Y), model) for t in totals], axis=1
        )

    partial_pre, chosen = lax.optimization_barrier((encode(0, early), chosen))
    pre_acts, x[early] = lax.optimization_barrier((sum_tok(partial_pre), x[early]))
    activation = list(act(pre_acts, 0, early))
    sent = by_plane([decode(u, range(u + 1)) for u in range(early)])
    sent, partial_pre, begun = lax.optimization_barrier(
        (sent, encode(early, layers), decode(early, range(early)))
    )
    summed_early = scatter_plane(sent)
    activation += list(act(sum_tok(partial_pre), early, layers))
    sent = by_plane([begun + decode(early, [early])])
    sent, summed_early = lax.optimization_barrier((sent, summed_early))
    summed = scatter_z(jnp.concatenate([summed_early, scatter_plane(sent)]))
    summed = summed + decoder_bias[:, None, :]
    recon = summed.astype(bf16)
    errors_home = (summed - targets.astype(f32)).astype(bf16)
    errors_got = gather_plane(gather_z(errors_home))
    errors_all = [errors_got[:, l].reshape(tokens, model) for l in range(layers)]
    partial_grad = []
    for source in range(layers):
        grad_act = None
        for target_layer in range(source, layers):
            product = lax.dot_general(
                errors_all[target_layer],
                decoder_weight[pair_number(source, target_layer, layers)],
                (((1,), (1,)), ((), ())),
                preferred_element_type=f32,
            )
            grad_act = product if grad_act is None else grad_act + product
        partial_grad.append(grad_act)
    partial_grad = jnp.stack(partial_grad)
    both, errors_got = lax.optimization_barrier((swap(partial_grad, "core"), errors_got))
    both = (partial_grad + both).astype(bf16)
    errors_all = [errors_got[:, l].reshape(tokens, model) for l in range(layers)]
    decoder_grads = [
        lax.dot_general(
            activation[source],
            errors_all[target_layer],
            (((0,), (0,)), ((), ())),
            preferred_element_type=f32,
        ).astype(bf16)
        for source in range(layers)
        for target_layer in range(source, layers)
    ]
    grad_act_all = both.astype(f32) + swap(both, "xl").astype(f32)
    grad_pre = jnp.where(chosen, grad_act_all, 0.0).astype(bf16)
    encoder_grad = jnp.stack(
        [
            lax.dot_general(
                x[l], grad_pre[l], (((0,), (0,)), ((), ())), preferred_element_type=f32
            ).astype(bf16)
            for l in range(layers)
        ]
    )
    encoder_bias_grad = jnp.sum(grad_pre.astype(f32), axis=1)
    decoder_bias_grad = jnp.sum(errors_got.astype(f32), axis=(0, 2))
    return (recon, encoder_grad, encoder_bias_grad, jnp.stack(decoder_grads), decoder_bias_grad)


def solution(mesh):
    fine = Mesh(mesh.devices.reshape(XH, Z, Y, XL, CORE), FEAT + TOK)
    in_specs = (
        P(None, FEAT, TOK),
        P(None, FEAT, TOK),
        P(),
        P(None, TOK, FEAT),
        P(None, FEAT),
        P(None, FEAT, TOK),
        P(None, TOK),
    )
    out_specs = (
        P(None, FEAT, TOK),
        P(None, TOK, FEAT),
        P(None, FEAT),
        P(None, FEAT, TOK),
        P(None, TOK),
    )
    return jax.shard_map(body, mesh=fine, in_specs=in_specs, out_specs=out_specs, check_vma=False)
```

```python
import jax
import jax.numpy as jnp
from jax import lax
from jax.experimental import pallas as pl
from jax.experimental.pallas import tpu as pltpu
from jax.sharding import Mesh, PartitionSpec as P

FEAT = ("xh", "z", "y")
TOK = ("xl", "core")
PLANE = ("xh", "y")
XH, Z, Y, XL, CORE = 2, 16, 4, 2, 2
bf16, f32 = jnp.bfloat16, jnp.float32


def pair_number(source, target_layer, layers):
    return sum((layers - before for before in range(source))) + target_layer - source


def swap(x, axis):
    return lax.ppermute(x, axis, [(0, 1), (1, 0)])


def gather_z(home):
    layers, rows, width = home.shape
    return lax.all_to_all(jnp.broadcast_to(home[None], (Z, layers, rows, width)), "z", 0, 0)


def gather_plane(along_z):
    _, layers, rows, width = along_z.shape
    block = along_z.transpose(1, 0, 2, 3).reshape(1, layers, Z * rows, width)
    return lax.all_to_all(
        jnp.broadcast_to(block, (XH * Y,) + block.shape[1:]), PLANE, 0, 0
    )


def scatter_tokens(sent):
    planes, layers, rows, width = sent.shape
    got = lax.all_to_all(sent, PLANE, 0, 0)
    summed = jnp.sum(got.astype(f32), axis=0).astype(bf16)
    blocks = summed.reshape(layers, Z, rows // Z, width).transpose(1, 0, 2, 3)
    got = lax.all_to_all(blocks, "z", 0, 0)
    return jnp.sum(got.astype(f32), axis=0)


def rows_of(ref, layer):
    block = ref[:, layer]
    return block.reshape(block.shape[0] * block.shape[1], block.shape[2])


def encode_kernel(x_ref, weight_ref, out_ref):
    for l in range(out_ref.shape[0]):
        out_ref[l] = jnp.dot(rows_of(x_ref, l), weight_ref[l], preferred_element_type=f32)


def decode_kernel(mine_ref, theirs_ref, bias_ref, mask_ref, weight_ref, act_ref, out_ref):
    layers = act_ref.shape[0]
    for l in range(layers):
        pre_acts = mine_ref[l].astype(f32) + theirs_ref[l].astype(f32) + bias_ref[l : l + 1]
        act_ref[l] = jnp.where(mask_ref[l] != 0, pre_acts, 0.0).astype(bf16)
    for u in range(layers):
        totals = None
        for s in range(u + 1):
            product = jnp.dot(
                act_ref[s], weight_ref[pair_number(s, u, layers)], preferred_element_type=f32
            )
            totals = product if totals is None else totals + product
        out_ref[:, u] = totals.astype(bf16).reshape(
            out_ref.shape[0], out_ref.shape[2], out_ref.shape[3]
        )


def grad_kernel(errors_ref, weight_ref, out_ref):
    layers = out_ref.shape[0]
    for s in range(layers):
        grad_act = None
        for u in range(s, layers):
            product = lax.dot_general(
                rows_of(errors_ref, u),
                weight_ref[pair_number(s, u, layers)],
                (((1,), (1,)), ((), ())),
                preferred_element_type=f32,
            )
            grad_act = product if grad_act is None else grad_act + product
        out_ref[s] = grad_act


def decoder_grad_kernel(act_ref, errors_ref, out_ref, bias_ref):
    layers = act_ref.shape[0]
    for u in range(layers):
        errors = rows_of(errors_ref, u)
        bias_ref[u : u + 1] = jnp.sum(errors.astype(f32), axis=0, keepdims=True)
        for s in range(u + 1):
            out_ref[pair_number(s, u, layers)] = lax.dot_general(
                act_ref[s], errors, (((0,), (0,)), ((), ())), preferred_element_type=f32
            ).astype(bf16)


def encoder_grad_kernel(mine_ref, theirs_ref, mask_ref, x_ref, out_ref, bias_ref):
    for l in range(out_ref.shape[0]):
        grad_act = mine_ref[l].astype(f32) + theirs_ref[l].astype(f32)
        grad_pre = jnp.where(mask_ref[l] != 0, grad_act, 0.0).astype(bf16)
        bias_ref[l : l + 1] = jnp.sum(grad_pre.astype(f32), axis=0, keepdims=True)
        out_ref[l] = lax.dot_general(
            rows_of(x_ref, l), grad_pre, (((0,), (0,)), ((), ())), preferred_element_type=f32
        ).astype(bf16)


def call(kernel, args, outs, flops):
    size = sum(a.size * a.dtype.itemsize for a in args)
    return pl.pallas_call(
        kernel,
        out_shape=[jax.ShapeDtypeStruct(shape, kind) for shape, kind in outs],
        in_specs=[pl.BlockSpec(memory_space=pltpu.VMEM) for _ in args],
        out_specs=[pl.BlockSpec(memory_space=pltpu.VMEM) for _ in outs],
        compiler_params=pltpu.CompilerParams(vmem_limit_bytes=24 << 20),
        cost_estimate=pl.CostEstimate(flops=flops, bytes_accessed=2 * size, transcendentals=0),
    )(*args)


def body(
    layer_inputs, targets, winners, encoder_weight, encoder_bias, decoder_weight, decoder_bias
):
    layers = layer_inputs.shape[0]
    width_here = encoder_weight.shape[2]
    picks = winners.shape[2]
    tokens = winners.shape[1]
    model = encoder_weight.shape[1]

    along_z = gather_z(layer_inputs)

    order = winners.reshape(layers, XH, Z, Y, 2, picks).transpose(0, 1, 3, 2, 4, 5)
    order = order.reshape(layers, tokens, picks)
    feature_ids = lax.axis_index(FEAT) * width_here + jnp.arange(width_here, dtype=jnp.int32)
    chosen = jnp.zeros((layers, tokens, width_here), jnp.bool_)
    for offset in range(0, picks, 8):
        matches = order[:, :, offset : offset + 8, None] == feature_ids
        chosen = jnp.logical_or(chosen, jnp.any(matches, axis=2))
    along_z, chosen = lax.optimization_barrier((along_z, chosen.astype(bf16)))
    gathered = gather_plane(along_z)

    planes, rows = XH * Y, tokens // (XH * Y)
    narrow = (layers, tokens, width_here)
    work = 2 * tokens * width_here * model
    (partial_pre,) = call(
        encode_kernel, (gathered, encoder_weight), [(narrow, f32)], layers * work
    )
    mine = (partial_pre + swap(partial_pre, "core")).astype(bf16)
    activation, sent = call(
        decode_kernel,
        (mine, swap(mine, "xl"), encoder_bias, chosen, decoder_weight),
        [(narrow, bf16), ((planes, layers, rows, model), bf16)],
        decoder_weight.shape[0] * work,
    )
    summed = scatter_tokens(sent) + decoder_bias[:, None, :]
    recon = summed.astype(bf16)
    errors_home = (summed - targets.astype(f32)).astype(bf16)
    errors_got = gather_plane(gather_z(errors_home))
    (partial_grad,) = call(
        grad_kernel,
        (errors_got, decoder_weight),
        [(narrow, f32)],
        decoder_weight.shape[0] * work,
    )
    both, errors_got = lax.optimization_barrier((swap(partial_grad, "core"), errors_got))
    mine = (partial_grad + both).astype(bf16)
    decoder_grad, decoder_bias_grad = call(
        decoder_grad_kernel,
        (activation, errors_got),
        [(decoder_weight.shape, bf16), ((layers, model), f32)],
        decoder_weight.shape[0] * work,
    )
    encoder_grad, encoder_bias_grad = call(
        encoder_grad_kernel,
        (mine, swap(mine, "xl"), chosen, gathered),
        [((layers, model, width_here), bf16), ((layers, width_here), f32)],
        layers * work,
    )
    return (recon, encoder_grad, encoder_bias_grad, decoder_grad, decoder_bias_grad)


def solution(mesh):
    fine = Mesh(mesh.devices.reshape(XH, Z, Y, XL, CORE), FEAT + TOK)
    in_specs = (
        P(None, FEAT, TOK),
        P(None, FEAT, TOK),
        P(),
        P(None, TOK, FEAT),
        P(None, FEAT),
        P(None, FEAT, TOK),
        P(None, TOK),
    )
    out_specs = (
        P(None, FEAT, TOK),
        P(None, TOK, FEAT),
        P(None, FEAT),
        P(None, FEAT, TOK),
        P(None, TOK),
    )
    return jax.shard_map(body, mesh=fine, in_specs=in_specs, out_specs=out_specs, check_vma=False)
```

```python
import jax
import jax.numpy as jnp
from jax import lax
from jax.experimental import pallas as pl
from jax.experimental.pallas import tpu as pltpu
from jax.sharding import Mesh, PartitionSpec as P

FEAT = ("xh", "z", "y")
TOK = ("xl", "core")
PLANE = ("xh", "y")
XH, Z, Y, XL, CORE = 2, 16, 4, 2, 2
VMEM_BYTES = 8 << 20
bf16, f32 = jnp.bfloat16, jnp.float32


def pair_number(source, target_layer, layers):
    return sum((layers - before for before in range(source))) + target_layer - source


def swap(x, axis):
    return lax.ppermute(x, axis, [(0, 1), (1, 0)])


def gather_z(home):
    return lax.all_to_all(jnp.broadcast_to(home[None], (Z,) + home.shape), "z", 0, 0)


def spread_kernel(along_z_ref, out_ref, rows_ref):
    columns, layers, rows, _ = along_z_ref.shape
    for l in range(layers):
        for z in range(columns):
            rows_ref[z * rows : (z + 1) * rows] = along_z_ref[z, l].astype(f32)
        block = rows_ref[...].astype(bf16)
        for p in range(out_ref.shape[0]):
            out_ref[p, l] = block


def gather_plane(along_z):
    columns, layers, rows, width = along_z.shape
    (block,) = call(
        spread_kernel,
        (along_z,),
        [((XH * Y, layers, columns * rows, width), bf16)],
        along_z.size,
        [pltpu.VMEM((columns * rows, width), f32)],
    )
    return lax.all_to_all(block, PLANE, 0, 0)


def plane_sum_kernel(got_ref, out_ref, rows_ref):
    columns, layers, rows, _ = out_ref.shape
    for l in range(layers):
        total = got_ref[0, l].astype(f32)
        for p in range(1, got_ref.shape[0]):
            total = total + got_ref[p, l].astype(f32)
        rows_ref[...] = total
        for z in range(columns):
            out_ref[z, l] = rows_ref[z * rows : (z + 1) * rows].astype(bf16)


def errors_kernel(got_ref, bias_ref, targets_ref, recon_ref, out_ref):
    columns, layers = got_ref.shape[:2]
    for l in range(layers):
        total = got_ref[0, l].astype(f32)
        for z in range(1, columns):
            total = total + got_ref[z, l].astype(f32)
        total = total + bias_ref[l : l + 1]
        recon_ref[l] = total.astype(bf16)
        errors = (total - targets_ref[l].astype(f32)).astype(bf16)
        for z in range(columns):
            out_ref[z, l] = errors


def rows_of(ref, layer):
    block = ref[:, layer]
    return block.reshape(block.shape[0] * block.shape[1], block.shape[2])


def encode_kernel(x_ref, weight_ref, out_ref):
    for l in range(out_ref.shape[0]):
        out_ref[l] = jnp.dot(rows_of(x_ref, l), weight_ref[l], preferred_element_type=f32)


def decode_kernel(mine_ref, theirs_ref, bias_ref, mask_ref, weight_ref, act_ref, out_ref):
    layers = act_ref.shape[0]
    for l in range(layers):
        pre_acts = mine_ref[l].astype(f32) + theirs_ref[l].astype(f32) + bias_ref[l : l + 1]
        act_ref[l] = jnp.where(mask_ref[l] != 0, pre_acts, 0.0).astype(bf16)
    for u in range(layers):
        totals = None
        for s in range(u + 1):
            product = jnp.dot(
                act_ref[s], weight_ref[pair_number(s, u, layers)], preferred_element_type=f32
            )
            totals = product if totals is None else totals + product
        out_ref[:, u] = totals.astype(bf16).reshape(
            out_ref.shape[0], out_ref.shape[2], out_ref.shape[3]
        )


def grad_kernel(errors_ref, weight_ref, out_ref):
    layers = out_ref.shape[0]
    for s in range(layers):
        grad_act = None
        for u in range(s, layers):
            product = lax.dot_general(
                rows_of(errors_ref, u),
                weight_ref[pair_number(s, u, layers)],
                (((1,), (1,)), ((), ())),
                preferred_element_type=f32,
            )
            grad_act = product if grad_act is None else grad_act + product
        out_ref[s] = grad_act


def decoder_grad_kernel(act_ref, errors_ref, out_ref, bias_ref):
    layers = act_ref.shape[0]
    for u in range(layers):
        errors = rows_of(errors_ref, u)
        bias_ref[u : u + 1] = jnp.sum(errors.astype(f32), axis=0, keepdims=True)
        for s in range(u + 1):
            out_ref[pair_number(s, u, layers)] = lax.dot_general(
                act_ref[s], errors, (((0,), (0,)), ((), ())), preferred_element_type=f32
            ).astype(bf16)


def encoder_grad_kernel(mine_ref, theirs_ref, mask_ref, x_ref, out_ref, bias_ref):
    for l in range(out_ref.shape[0]):
        grad_act = mine_ref[l].astype(f32) + theirs_ref[l].astype(f32)
        grad_pre = jnp.where(mask_ref[l] != 0, grad_act, 0.0).astype(bf16)
        bias_ref[l : l + 1] = jnp.sum(grad_pre.astype(f32), axis=0, keepdims=True)
        out_ref[l] = lax.dot_general(
            rows_of(x_ref, l), grad_pre, (((0,), (0,)), ((), ())), preferred_element_type=f32
        ).astype(bf16)


def call(kernel, args, outs, flops, scratch=()):
    size = sum(a.size * a.dtype.itemsize for a in args)
    return pl.pallas_call(
        kernel,
        out_shape=[jax.ShapeDtypeStruct(shape, kind) for shape, kind in outs],
        in_specs=[pl.BlockSpec(memory_space=pltpu.VMEM) for _ in args],
        out_specs=[pl.BlockSpec(memory_space=pltpu.VMEM) for _ in outs],
        scratch_shapes=list(scratch),
        compiler_params=pltpu.CompilerParams(vmem_limit_bytes=VMEM_BYTES),
        cost_estimate=pl.CostEstimate(flops=flops, bytes_accessed=2 * size, transcendentals=0),
    )(*args)


def body(
    layer_inputs, targets, winners, encoder_weight, encoder_bias, decoder_weight, decoder_bias
):
    layers = layer_inputs.shape[0]
    width_here = encoder_weight.shape[2]
    picks = winners.shape[2]
    tokens = winners.shape[1]
    model = encoder_weight.shape[1]

    along_z = gather_z(layer_inputs)

    order = winners.reshape(layers, XH, Z, Y, 2, picks).transpose(0, 1, 3, 2, 4, 5)
    order = order.reshape(layers, tokens, picks)
    feature_ids = lax.axis_index(FEAT) * width_here + jnp.arange(width_here, dtype=jnp.int32)
    chosen = jnp.zeros((layers, tokens, width_here), jnp.bool_)
    for offset in range(0, picks, 8):
        matches = order[:, :, offset : offset + 8, None] == feature_ids
        chosen = jnp.logical_or(chosen, jnp.any(matches, axis=2))
    gathered, chosen = lax.optimization_barrier((gather_plane(along_z), chosen.astype(bf16)))

    planes, rows = XH * Y, tokens // (XH * Y)
    narrow = (layers, tokens, width_here)
    work = 2 * tokens * width_here * model
    (partial_pre,) = call(
        encode_kernel, (gathered, encoder_weight), [(narrow, f32)], layers * work
    )
    mine = (partial_pre + swap(partial_pre, "core")).astype(bf16)
    activation, sent = call(
        decode_kernel,
        (mine, swap(mine, "xl"), encoder_bias, chosen, decoder_weight),
        [(narrow, bf16), ((planes, layers, rows, model), bf16)],
        decoder_weight.shape[0] * work,
    )
    columns = (Z, layers, rows // Z, model)
    (blocks,) = call(
        plane_sum_kernel,
        (lax.all_to_all(sent, PLANE, 0, 0),),
        [(columns, bf16)],
        sent.size,
        [pltpu.VMEM((rows, model), f32)],
    )
    recon, errors_home = call(
        errors_kernel,
        (lax.all_to_all(blocks, "z", 0, 0), decoder_bias, targets),
        [(targets.shape, bf16), (columns, bf16)],
        blocks.size,
    )
    errors_got = gather_plane(lax.all_to_all(errors_home, "z", 0, 0))
    (partial_grad,) = call(
        grad_kernel,
        (errors_got, decoder_weight),
        [(narrow, f32)],
        decoder_weight.shape[0] * work,
    )
    both, errors_got = lax.optimization_barrier((swap(partial_grad, "core"), errors_got))
    mine = (partial_grad + both).astype(bf16)
    decoder_grad, decoder_bias_grad = call(
        decoder_grad_kernel,
        (activation, errors_got),
        [(decoder_weight.shape, bf16), ((layers, model), f32)],
        decoder_weight.shape[0] * work,
    )
    encoder_grad, encoder_bias_grad = call(
        encoder_grad_kernel,
        (mine, swap(mine, "xl"), chosen, gathered),
        [((layers, model, width_here), bf16), ((layers, width_here), f32)],
        layers * work,
    )
    return (recon, encoder_grad, encoder_bias_grad, decoder_grad, decoder_bias_grad)


def solution(mesh):
    fine = Mesh(mesh.devices.reshape(XH, Z, Y, XL, CORE), FEAT + TOK)
    in_specs = (
        P(None, FEAT, TOK),
        P(None, FEAT, TOK),
        P(),
        P(None, TOK, FEAT),
        P(None, FEAT),
        P(None, FEAT, TOK),
        P(None, TOK),
    )
    out_specs = (
        P(None, FEAT, TOK),
        P(None, TOK, FEAT),
        P(None, FEAT),
        P(None, FEAT, TOK),
        P(None, TOK),
    )
    return jax.shard_map(body, mesh=fine, in_specs=in_specs, out_specs=out_specs, check_vma=False)
```

```python
import jax
import jax.numpy as jnp
from jax import lax
from jax.experimental import pallas as pl
from jax.experimental.pallas import tpu as pltpu
from jax.sharding import Mesh, PartitionSpec as P

FEAT = ("xh", "z", "y")
TOK = ("xl", "core")
PLANE = ("xh", "y")
XH, Z, Y, XL, CORE = 2, 16, 4, 2, 2
VMEM_BYTES = 8 << 20
bf16, f32 = jnp.bfloat16, jnp.float32


def pair_number(source, target_layer, layers):
    return sum((layers - before for before in range(source))) + target_layer - source


def swap(x, axis):
    return lax.ppermute(x, axis, [(0, 1), (1, 0)])


def copies_kernel(home_ref, out_ref):
    for z in range(out_ref.shape[0]):
        out_ref[z] = home_ref[...]


def gather_z(home):
    (copies,) = call(copies_kernel, (home,), [((Z,) + home.shape, bf16)], home.size)
    return lax.all_to_all(copies, "z", 0, 0)


def spread_kernel(along_z_ref, out_ref, rows_ref):
    columns, layers, rows, _ = along_z_ref.shape
    for l in range(layers):
        for z in range(columns):
            rows_ref[z * rows : (z + 1) * rows] = along_z_ref[z, l].astype(f32)
        block = rows_ref[...].astype(bf16)
        for p in range(out_ref.shape[0]):
            out_ref[p, l] = block


def gather_plane(along_z):
    columns, layers, rows, width = along_z.shape
    (block,) = call(
        spread_kernel,
        (along_z,),
        [((XH * Y, layers, columns * rows, width), bf16)],
        along_z.size,
        [pltpu.VMEM((columns * rows, width), f32)],
    )
    return lax.all_to_all(block, PLANE, 0, 0)


def plane_sum_kernel(got_ref, out_ref, rows_ref):
    columns, layers, rows, _ = out_ref.shape
    for l in range(layers):
        total = got_ref[0, l].astype(f32)
        for p in range(1, got_ref.shape[0]):
            total = total + got_ref[p, l].astype(f32)
        rows_ref[...] = total
        for z in range(columns):
            out_ref[z, l] = rows_ref[z * rows : (z + 1) * rows].astype(bf16)


def errors_kernel(got_ref, bias_ref, targets_ref, recon_ref, out_ref):
    columns, layers = got_ref.shape[:2]
    for l in range(layers):
        total = got_ref[0, l].astype(f32)
        for z in range(1, columns):
            total = total + got_ref[z, l].astype(f32)
        total = total + bias_ref[l : l + 1]
        recon_ref[l] = total.astype(bf16)
        errors = (total - targets_ref[l].astype(f32)).astype(bf16)
        for z in range(columns):
            out_ref[z, l] = errors


def rows_of(ref, layer):
    block = ref[:, layer]
    return block.reshape(block.shape[0] * block.shape[1], block.shape[2])


def mask_kernel(winners_ref, out_ref, marks_ref):
    layers, picks, tokens = winners_ref.shape
    features = out_ref.shape[2]
    half = features // 2
    for l in range(layers):
        for h in range(0, features, half):
            ids = h + lax.broadcasted_iota(jnp.int32, (half, tokens), 0)
            marks = jnp.zeros((half, tokens), f32)
            for k in range(picks):
                marks = jnp.where(winners_ref[l, k : k + 1, :] == ids, 1.0, marks)
            marks_ref[h : h + half] = marks
        out_ref[l] = marks_ref[...].T.astype(bf16)


def encode_kernel(x_ref, weight_ref, out_ref):
    for l in range(out_ref.shape[0]):
        out_ref[l] = jnp.dot(rows_of(x_ref, l), weight_ref[l], preferred_element_type=f32)


def decode_kernel(mine_ref, theirs_ref, bias_ref, mask_ref, weight_ref, act_ref, out_ref):
    layers = act_ref.shape[0]
    for l in range(layers):
        pre_acts = mine_ref[l].astype(f32) + theirs_ref[l].astype(f32) + bias_ref[l : l + 1]
        act_ref[l] = jnp.where(mask_ref[l] != 0, pre_acts, 0.0).astype(bf16)
    for u in range(layers):
        totals = None
        for s in range(u + 1):
            product = jnp.dot(
                act_ref[s], weight_ref[pair_number(s, u, layers)], preferred_element_type=f32
            )
            totals = product if totals is None else totals + product
        out_ref[:, u] = totals.astype(bf16).reshape(
            out_ref.shape[0], out_ref.shape[2], out_ref.shape[3]
        )


def grad_kernel(errors_ref, weight_ref, out_ref):
    layers = out_ref.shape[0]
    for s in range(layers):
        grad_act = None
        for u in range(s, layers):
            product = lax.dot_general(
                rows_of(errors_ref, u),
                weight_ref[pair_number(s, u, layers)],
                (((1,), (1,)), ((), ())),
                preferred_element_type=f32,
            )
            grad_act = product if grad_act is None else grad_act + product
        out_ref[s] = grad_act


def decoder_grad_kernel(act_ref, errors_ref, x_ref, out_ref, bias_ref, turned_ref):
    layers = act_ref.shape[0]
    for l in range(layers):
        turned_ref[l] = rows_of(x_ref, l).T
    for u in range(layers):
        errors = rows_of(errors_ref, u)
        bias_ref[u : u + 1] = jnp.sum(errors.astype(f32), axis=0, keepdims=True)
        for s in range(u + 1):
            out_ref[pair_number(s, u, layers)] = lax.dot_general(
                act_ref[s], errors, (((0,), (0,)), ((), ())), preferred_element_type=f32
            ).astype(bf16)


def encoder_grad_kernel(mine_ref, theirs_ref, mask_ref, turned_ref, out_ref, bias_ref):
    for l in range(out_ref.shape[0]):
        grad_act = mine_ref[l].astype(f32) + theirs_ref[l].astype(f32)
        grad_pre = jnp.where(mask_ref[l] != 0, grad_act, 0.0).astype(bf16)
        bias_ref[l : l + 1] = jnp.sum(grad_pre.astype(f32), axis=0, keepdims=True)
        out_ref[l] = jnp.dot(
            turned_ref[l], grad_pre, preferred_element_type=f32
        ).astype(bf16)


def call(kernel, args, outs, flops, scratch=()):
    size = sum(a.size * a.dtype.itemsize for a in args)
    return pl.pallas_call(
        kernel,
        out_shape=[jax.ShapeDtypeStruct(shape, kind) for shape, kind in outs],
        in_specs=[pl.BlockSpec(memory_space=pltpu.VMEM) for _ in args],
        out_specs=[pl.BlockSpec(memory_space=pltpu.VMEM) for _ in outs],
        scratch_shapes=list(scratch),
        compiler_params=pltpu.CompilerParams(vmem_limit_bytes=VMEM_BYTES),
        cost_estimate=pl.CostEstimate(flops=flops, bytes_accessed=2 * size, transcendentals=0),
    )(*args)


def body(
    layer_inputs, targets, winners, encoder_weight, encoder_bias, decoder_weight, decoder_bias
):
    layers = layer_inputs.shape[0]
    width_here = encoder_weight.shape[2]
    picks = winners.shape[2]
    tokens = winners.shape[1]
    model = encoder_weight.shape[1]

    along_z = gather_z(layer_inputs)

    order = winners.reshape(layers, XH, Z, Y, 2, picks).transpose(0, 5, 1, 3, 2, 4)
    order = order.reshape(layers, picks, tokens) - lax.axis_index(FEAT) * width_here
    (chosen,) = call(
        mask_kernel,
        (order,),
        [((layers, tokens, width_here), bf16)],
        layers * picks * tokens * width_here,
        [pltpu.VMEM((width_here, tokens), f32)],
    )
    along_z, chosen = lax.optimization_barrier((along_z, chosen))
    gathered = gather_plane(along_z)

    planes, rows = XH * Y, tokens // (XH * Y)
    narrow = (layers, tokens, width_here)
    work = 2 * tokens * width_here * model
    (partial_pre,) = call(
        encode_kernel, (gathered, encoder_weight), [(narrow, f32)], layers * work
    )
    mine = (partial_pre + swap(partial_pre, "core")).astype(bf16)
    activation, sent = call(
        decode_kernel,
        (mine, swap(mine, "xl"), encoder_bias, chosen, decoder_weight),
        [(narrow, bf16), ((planes, layers, rows, model), bf16)],
        decoder_weight.shape[0] * work,
    )
    columns = (Z, layers, rows // Z, model)
    (blocks,) = call(
        plane_sum_kernel,
        (lax.all_to_all(sent, PLANE, 0, 0),),
        [(columns, bf16)],
        sent.size,
        [pltpu.VMEM((rows, model), f32)],
    )
    recon, errors_home = call(
        errors_kernel,
        (lax.all_to_all(blocks, "z", 0, 0), decoder_bias, targets),
        [(targets.shape, bf16), (columns, bf16)],
        blocks.size,
    )
    errors_got = gather_plane(lax.all_to_all(errors_home, "z", 0, 0))
    (partial_grad,) = call(
        grad_kernel,
        (errors_got, decoder_weight),
        [(narrow, f32)],
        decoder_weight.shape[0] * work,
    )
    both, errors_got = lax.optimization_barrier((swap(partial_grad, "core"), errors_got))
    mine = (partial_grad + both).astype(bf16)
    decoder_grad, decoder_bias_grad, turned = call(
        decoder_grad_kernel,
        (activation, errors_got, gathered),
        [(decoder_weight.shape, bf16), ((layers, model), f32), ((layers, model, tokens), bf16)],
        decoder_weight.shape[0] * work,
    )
    encoder_grad, encoder_bias_grad = call(
        encoder_grad_kernel,
        (mine, swap(mine, "xl"), chosen, turned),
        [((layers, model, width_here), bf16), ((layers, width_here), f32)],
        layers * work,
    )
    return (recon, encoder_grad, encoder_bias_grad, decoder_grad, decoder_bias_grad)


def solution(mesh):
    fine = Mesh(mesh.devices.reshape(XH, Z, Y, XL, CORE), FEAT + TOK)
    in_specs = (
        P(None, FEAT, TOK),
        P(None, FEAT, TOK),
        P(),
        P(None, TOK, FEAT),
        P(None, FEAT),
        P(None, FEAT, TOK),
        P(None, TOK),
    )
    out_specs = (
        P(None, FEAT, TOK),
        P(None, TOK, FEAT),
        P(None, FEAT),
        P(None, FEAT, TOK),
        P(None, TOK),
    )
    return jax.shard_map(body, mesh=fine, in_specs=in_specs, out_specs=out_specs, check_vma=False)
```

```python
import jax
import jax.numpy as jnp
from jax import lax
from jax.experimental import pallas as pl
from jax.experimental.pallas import tpu as pltpu
from jax.sharding import Mesh, PartitionSpec as P

FEAT = ("xh", "z", "y")
TOK = ("xl", "core")
PLANE = ("y", "xh")
XH, Z, Y, XL, CORE = 2, 16, 4, 2, 2
VMEM_BYTES = 8 << 20
bf16, f32 = jnp.bfloat16, jnp.float32


def pair_number(source, target_layer, layers):
    return sum((layers - before for before in range(source))) + target_layer - source


def swap(x, axis):
    return lax.ppermute(x, axis, [(0, 1), (1, 0)])


def copies_kernel(home_ref, out_ref):
    for z in range(out_ref.shape[0]):
        out_ref[z] = home_ref[...]


def gather_z(home):
    (copies,) = call(copies_kernel, (home,), [((Z,) + home.shape, bf16)], home.size)
    return lax.all_to_all(copies, "z", 0, 0)


def spread_kernel(along_z_ref, out_ref, rows_ref):
    columns, layers, rows, _ = along_z_ref.shape
    for l in range(layers):
        for z in range(columns):
            rows_ref[z * rows : (z + 1) * rows] = along_z_ref[z, l].astype(f32)
        block = rows_ref[...].astype(bf16)
        for p in range(out_ref.shape[0]):
            out_ref[p, l] = block


def gather_plane(along_z):
    columns, layers, rows, width = along_z.shape
    (block,) = call(
        spread_kernel,
        (along_z,),
        [((XH * Y, layers, columns * rows, width), bf16)],
        along_z.size,
        [pltpu.VMEM((columns * rows, width), f32)],
    )
    return lax.all_to_all(block, PLANE, 0, 0)


def plane_sum_kernel(got_ref, out_ref, rows_ref):
    columns, layers, rows, _ = out_ref.shape
    for l in range(layers):
        total = got_ref[0, l].astype(f32)
        for p in range(1, got_ref.shape[0]):
            total = total + got_ref[p, l].astype(f32)
        rows_ref[...] = total
        for z in range(columns):
            out_ref[z, l] = rows_ref[z * rows : (z + 1) * rows].astype(bf16)


def errors_kernel(got_ref, bias_ref, targets_ref, recon_ref, out_ref):
    columns, layers = got_ref.shape[:2]
    for l in range(layers):
        total = got_ref[0, l].astype(f32)
        for z in range(1, columns):
            total = total + got_ref[z, l].astype(f32)
        total = total + bias_ref[l : l + 1]
        recon_ref[l] = total.astype(bf16)
        errors = (total - targets_ref[l].astype(f32)).astype(bf16)
        for z in range(columns):
            out_ref[z, l] = errors


def rows_of(ref, layer):
    block = ref[:, layer]
    return block.reshape(block.shape[0] * block.shape[1], block.shape[2])


def mask_kernel(winners_ref, out_ref, marks_ref):
    layers, picks, tokens = winners_ref.shape
    features = out_ref.shape[2]
    half = features // 2
    for l in range(layers):
        for h in range(0, features, half):
            ids = h + lax.broadcasted_iota(jnp.int32, (half, tokens), 0)
            marks = jnp.zeros((half, tokens), f32)
            for k in range(picks):
                marks = jnp.where(winners_ref[l, k : k + 1, :] == ids, 1.0, marks)
            marks_ref[h : h + half] = marks
        out_ref[l] = marks_ref[...].T.astype(bf16)


def encode_kernel(x_ref, weight_ref, out_ref):
    for l in range(out_ref.shape[0]):
        out_ref[l] = jnp.dot(rows_of(x_ref, l), weight_ref[l], preferred_element_type=f32)


def decode_kernel(mine_ref, theirs_ref, bias_ref, mask_ref, weight_ref, act_ref, out_ref):
    layers = act_ref.shape[0]
    for l in range(layers):
        pre_acts = mine_ref[l].astype(f32) + theirs_ref[l].astype(f32) + bias_ref[l : l + 1]
        act_ref[l] = jnp.where(mask_ref[l] != 0, pre_acts, 0.0).astype(bf16)
    for u in range(layers):
        totals = None
        for s in range(u + 1):
            product = jnp.dot(
                act_ref[s], weight_ref[pair_number(s, u, layers)], preferred_element_type=f32
            )
            totals = product if totals is None else totals + product
        out_ref[:, u] = totals.astype(bf16).reshape(
            out_ref.shape[0], out_ref.shape[2], out_ref.shape[3]
        )


def grad_kernel(errors_ref, weight_ref, out_ref):
    layers = out_ref.shape[0]
    for s in range(layers):
        grad_act = None
        for u in range(s, layers):
            product = lax.dot_general(
                rows_of(errors_ref, u),
                weight_ref[pair_number(s, u, layers)],
                (((1,), (1,)), ((), ())),
                preferred_element_type=f32,
            )
            grad_act = product if grad_act is None else grad_act + product
        out_ref[s] = grad_act


def decoder_grad_kernel(act_ref, errors_ref, x_ref, out_ref, bias_ref, turned_ref):
    layers = act_ref.shape[0]
    for l in range(layers):
        turned_ref[l] = rows_of(x_ref, l).T
    for u in range(layers):
        errors = rows_of(errors_ref, u)
        bias_ref[u : u + 1] = jnp.sum(errors.astype(f32), axis=0, keepdims=True)
        for s in range(u + 1):
            out_ref[pair_number(s, u, layers)] = lax.dot_general(
                act_ref[s], errors, (((0,), (0,)), ((), ())), preferred_element_type=f32
            ).astype(bf16)


def encoder_grad_kernel(mine_ref, theirs_ref, mask_ref, turned_ref, out_ref, bias_ref):
    for l in range(out_ref.shape[0]):
        grad_act = mine_ref[l].astype(f32) + theirs_ref[l].astype(f32)
        grad_pre = jnp.where(mask_ref[l] != 0, grad_act, 0.0).astype(bf16)
        bias_ref[l : l + 1] = jnp.sum(grad_pre.astype(f32), axis=0, keepdims=True)
        out_ref[l] = jnp.dot(
            turned_ref[l], grad_pre, preferred_element_type=f32
        ).astype(bf16)


def call(kernel, args, outs, flops, scratch=()):
    size = sum(a.size * a.dtype.itemsize for a in args)
    return pl.pallas_call(
        kernel,
        out_shape=[jax.ShapeDtypeStruct(shape, kind) for shape, kind in outs],
        in_specs=[pl.BlockSpec(memory_space=pltpu.VMEM) for _ in args],
        out_specs=[pl.BlockSpec(memory_space=pltpu.VMEM) for _ in outs],
        scratch_shapes=list(scratch),
        compiler_params=pltpu.CompilerParams(vmem_limit_bytes=VMEM_BYTES),
        cost_estimate=pl.CostEstimate(flops=flops, bytes_accessed=2 * size, transcendentals=0),
    )(*args)


def body(
    layer_inputs, targets, winners, encoder_weight, encoder_bias, decoder_weight, decoder_bias
):
    layers = layer_inputs.shape[0]
    width_here = encoder_weight.shape[2]
    picks = winners.shape[2]
    tokens = winners.shape[1]
    model = encoder_weight.shape[1]

    along_z = gather_z(layer_inputs)

    order = winners.reshape(layers, XH, Z, Y, 2, picks).transpose(0, 5, 3, 1, 2, 4)
    order = order.reshape(layers, picks, tokens) - lax.axis_index(FEAT) * width_here
    (chosen,) = call(
        mask_kernel,
        (order,),
        [((layers, tokens, width_here), bf16)],
        layers * picks * tokens * width_here,
        [pltpu.VMEM((width_here, tokens), f32)],
    )
    along_z, chosen = lax.optimization_barrier((along_z, chosen))
    gathered = gather_plane(along_z)

    planes, rows = XH * Y, tokens // (XH * Y)
    narrow = (layers, tokens, width_here)
    work = 2 * tokens * width_here * model
    (partial_pre,) = call(
        encode_kernel, (gathered, encoder_weight), [(narrow, f32)], layers * work
    )
    mine = (partial_pre + swap(partial_pre, "core")).astype(bf16)
    activation, sent = call(
        decode_kernel,
        (mine, swap(mine, "xl"), encoder_bias, chosen, decoder_weight),
        [(narrow, bf16), ((planes, layers, rows, model), bf16)],
        decoder_weight.shape[0] * work,
    )
    columns = (Z, layers, rows // Z, model)
    (blocks,) = call(
        plane_sum_kernel,
        (lax.all_to_all(sent, PLANE, 0, 0),),
        [(columns, bf16)],
        sent.size,
        [pltpu.VMEM((rows, model), f32)],
    )
    recon, errors_home = call(
        errors_kernel,
        (lax.all_to_all(blocks, "z", 0, 0), decoder_bias, targets),
        [(targets.shape, bf16), (columns, bf16)],
        blocks.size,
    )
    errors_got = gather_plane(lax.all_to_all(errors_home, "z", 0, 0))
    (partial_grad,) = call(
        grad_kernel,
        (errors_got, decoder_weight),
        [(narrow, f32)],
        decoder_weight.shape[0] * work,
    )
    both, errors_got = lax.optimization_barrier((swap(partial_grad, "core"), errors_got))
    mine = (partial_grad + both).astype(bf16)
    decoder_grad, decoder_bias_grad, turned = call(
        decoder_grad_kernel,
        (activation, errors_got, gathered),
        [(decoder_weight.shape, bf16), ((layers, model), f32), ((layers, model, tokens), bf16)],
        decoder_weight.shape[0] * work,
    )
    encoder_grad, encoder_bias_grad = call(
        encoder_grad_kernel,
        (mine, swap(mine, "xl"), chosen, turned),
        [((layers, model, width_here), bf16), ((layers, width_here), f32)],
        layers * work,
    )
    return (recon, encoder_grad, encoder_bias_grad, decoder_grad, decoder_bias_grad)


def solution(mesh):
    fine = Mesh(mesh.devices.reshape(XH, Z, Y, XL, CORE), FEAT + TOK)
    in_specs = (
        P(None, FEAT, TOK),
        P(None, FEAT, TOK),
        P(),
        P(None, TOK, FEAT),
        P(None, FEAT),
        P(None, FEAT, TOK),
        P(None, TOK),
    )
    out_specs = (
        P(None, FEAT, TOK),
        P(None, TOK, FEAT),
        P(None, FEAT),
        P(None, FEAT, TOK),
        P(None, TOK),
    )
    return jax.shard_map(body, mesh=fine, in_specs=in_specs, out_specs=out_specs, check_vma=False)
```

```python
import jax
import jax.numpy as jnp
from jax import lax
from jax.experimental import pallas as pl
from jax.experimental.pallas import tpu as pltpu
from jax.sharding import Mesh, PartitionSpec as P

FEAT = ("xh", "z", "y")
TOK = ("xl", "core")
PLANE = ("y", "xh")
XH, Z, Y, XL, CORE = 2, 16, 4, 2, 2
VMEM_BYTES = 8 << 20
bf16, f32 = jnp.bfloat16, jnp.float32


def pair_number(source, target_layer, layers):
    return sum((layers - before for before in range(source))) + target_layer - source


def swap(x, axis):
    return lax.ppermute(x, axis, [(0, 1), (1, 0)])


def copies_kernel(home_ref, out_ref):
    for z in range(out_ref.shape[0]):
        out_ref[z] = home_ref[...]


def gather_z(home):
    (copies,) = call(copies_kernel, (home,), [((Z,) + home.shape, bf16)], home.size)
    return lax.all_to_all(copies, "z", 0, 0)


def spread_kernel(along_z_ref, out_ref, rows_ref):
    columns, layers, rows, _ = along_z_ref.shape
    for l in range(layers):
        for z in range(columns):
            rows_ref[z * rows : (z + 1) * rows] = along_z_ref[z, l].astype(f32)
        block = rows_ref[...].astype(bf16)
        for p in range(out_ref.shape[0]):
            out_ref[p, l] = block


def gather_plane(along_z):
    columns, layers, rows, width = along_z.shape
    (block,) = call(
        spread_kernel,
        (along_z,),
        [((XH * Y, layers, columns * rows, width), bf16)],
        along_z.size,
        [pltpu.VMEM((columns * rows, width), f32)],
    )
    return lax.all_to_all(block, PLANE, 0, 0)


def plane_sum_kernel(got_ref, out_ref, rows_ref):
    columns, layers, rows, _ = out_ref.shape
    for l in range(layers):
        total = got_ref[0, l].astype(f32)
        for p in range(1, got_ref.shape[0]):
            total = total + got_ref[p, l].astype(f32)
        rows_ref[...] = total
        for z in range(columns):
            out_ref[z, l] = rows_ref[z * rows : (z + 1) * rows].astype(bf16)


def errors_kernel(got_ref, bias_ref, targets_ref, recon_ref, out_ref):
    columns, layers = got_ref.shape[:2]
    for l in range(layers):
        total = got_ref[0, l].astype(f32)
        for z in range(1, columns):
            total = total + got_ref[z, l].astype(f32)
        total = total + bias_ref[l : l + 1]
        recon_ref[l] = total.astype(bf16)
        errors = (total - targets_ref[l].astype(f32)).astype(bf16)
        for z in range(columns):
            out_ref[z, l] = errors


def rows_of(ref, layer):
    block = ref[:, layer]
    return block.reshape(block.shape[0] * block.shape[1], block.shape[2])


def mask_kernel(winners_ref, slot_ref, pick_ref, marks_ref):
    layers, picks, tokens = winners_ref.shape
    features = slot_ref.shape[2]
    half, near = features // 2, tokens // 2
    for l in range(layers):
        for h in range(0, features, half):
            ids = h + lax.broadcasted_iota(jnp.int32, (half, tokens), 0)
            marks = jnp.zeros((half, tokens), f32)
            for k in range(picks):
                marks = jnp.where(winners_ref[l, k : k + 1, :] == ids, float(k + 1), marks)
            marks_ref[h : h + half] = marks
        slot_ref[l] = marks_ref[...].T.astype(jnp.int32)
        here = jnp.clip(winners_ref[l], 0, features - 1).astype(f32)
        marks_ref[:picks, :near] = here[:, :near]
        marks_ref[picks : 2 * picks, :near] = here[:, near:]
        pick_ref[l] = marks_ref[:, :near].T.astype(jnp.int32)


def take(values, places):
    return jnp.take_along_axis(values, places, axis=1, mode="promise_in_bounds")


def pack(values, pick):
    near, lanes = pick.shape
    first = lax.broadcasted_iota(jnp.int32, (near, lanes), 1) < lanes // 2
    return jnp.where(first, take(values[:near], pick), take(values[near:], pick))


def unpack(packed, slot_ref, layer):
    near, lanes = packed.shape
    for part in range(2):
        rows = slice(part * near, (part + 1) * near)
        slot = slot_ref[layer, rows]
        place = jnp.maximum(slot - 1, 0) + part * (lanes // 2)
        yield rows, slot > 0, take(packed, place)


def encode_kernel(x_ref, weight_ref, pick_ref, out_ref):
    for l in range(out_ref.shape[0]):
        pre_acts = jnp.dot(rows_of(x_ref, l), weight_ref[l], preferred_element_type=f32)
        out_ref[l] = pack(pre_acts, pick_ref[l])


def decode_kernel(mine_ref, theirs_ref, bias_ref, slot_ref, weight_ref, act_ref, out_ref):
    layers = act_ref.shape[0]
    for l in range(layers):
        packed = mine_ref[l].astype(f32) + theirs_ref[l].astype(f32)
        for rows, chosen, values in unpack(packed, slot_ref, l):
            pre_acts = values + bias_ref[l : l + 1]
            act_ref[l, rows] = jnp.where(chosen, pre_acts, 0.0).astype(bf16)
    for u in range(layers):
        totals = None
        for s in range(u + 1):
            product = jnp.dot(
                act_ref[s], weight_ref[pair_number(s, u, layers)], preferred_element_type=f32
            )
            totals = product if totals is None else totals + product
        out_ref[:, u] = totals.astype(bf16).reshape(
            out_ref.shape[0], out_ref.shape[2], out_ref.shape[3]
        )


def grad_kernel(errors_ref, weight_ref, pick_ref, out_ref):
    layers = out_ref.shape[0]
    for s in range(layers):
        grad_act = None
        for u in range(s, layers):
            product = lax.dot_general(
                rows_of(errors_ref, u),
                weight_ref[pair_number(s, u, layers)],
                (((1,), (1,)), ((), ())),
                preferred_element_type=f32,
            )
            grad_act = product if grad_act is None else grad_act + product
        out_ref[s] = pack(grad_act, pick_ref[s])


def decoder_grad_kernel(act_ref, errors_ref, x_ref, out_ref, bias_ref, turned_ref):
    layers = act_ref.shape[0]
    for l in range(layers):
        turned_ref[l] = rows_of(x_ref, l).T
    for u in range(layers):
        errors = rows_of(errors_ref, u)
        bias_ref[u : u + 1] = jnp.sum(errors.astype(f32), axis=0, keepdims=True)
        for s in range(u + 1):
            out_ref[pair_number(s, u, layers)] = lax.dot_general(
                act_ref[s], errors, (((0,), (0,)), ((), ())), preferred_element_type=f32
            ).astype(bf16)


def encoder_grad_kernel(mine_ref, theirs_ref, slot_ref, turned_ref, out_ref, bias_ref, grad_ref):
    for l in range(out_ref.shape[0]):
        packed = mine_ref[l].astype(f32) + theirs_ref[l].astype(f32)
        for rows, chosen, values in unpack(packed, slot_ref, l):
            grad_ref[rows] = jnp.where(chosen, values, 0.0).astype(bf16)
        grad_pre = grad_ref[...]
        bias_ref[l : l + 1] = jnp.sum(grad_pre.astype(f32), axis=0, keepdims=True)
        out_ref[l] = jnp.dot(
            turned_ref[l], grad_pre, preferred_element_type=f32
        ).astype(bf16)


def call(kernel, args, outs, flops, scratch=()):
    size = sum(a.size * a.dtype.itemsize for a in args)
    return pl.pallas_call(
        kernel,
        out_shape=[jax.ShapeDtypeStruct(shape, kind) for shape, kind in outs],
        in_specs=[pl.BlockSpec(memory_space=pltpu.VMEM) for _ in args],
        out_specs=[pl.BlockSpec(memory_space=pltpu.VMEM) for _ in outs],
        scratch_shapes=list(scratch),
        compiler_params=pltpu.CompilerParams(vmem_limit_bytes=VMEM_BYTES),
        cost_estimate=pl.CostEstimate(flops=flops, bytes_accessed=2 * size, transcendentals=0),
    )(*args)


def body(
    layer_inputs, targets, winners, encoder_weight, encoder_bias, decoder_weight, decoder_bias
):
    layers = layer_inputs.shape[0]
    width_here = encoder_weight.shape[2]
    picks = winners.shape[2]
    tokens = winners.shape[1]
    model = encoder_weight.shape[1]

    along_z = gather_z(layer_inputs)

    order = winners.reshape(layers, XH, Z, Y, 2, picks).transpose(0, 5, 3, 1, 2, 4)
    order = order.reshape(layers, picks, tokens) - lax.axis_index(FEAT) * width_here
    slots, picked = call(
        mask_kernel,
        (order,),
        [
            ((layers, tokens, width_here), jnp.int32),
            ((layers, tokens // 2, 2 * picks), jnp.int32),
        ],
        layers * picks * tokens * width_here,
        [pltpu.VMEM((width_here, tokens), f32)],
    )
    along_z, slots, picked = lax.optimization_barrier((along_z, slots, picked))
    gathered = gather_plane(along_z)

    planes, rows = XH * Y, tokens // (XH * Y)
    narrow = (layers, tokens, width_here)
    packed = (layers, tokens // 2, 2 * picks)
    work = 2 * tokens * width_here * model
    (partial_pre,) = call(
        encode_kernel, (gathered, encoder_weight, picked), [(packed, f32)], layers * work
    )
    mine = (partial_pre + swap(partial_pre, "core")).astype(bf16)
    activation, sent = call(
        decode_kernel,
        (mine, swap(mine, "xl"), encoder_bias, slots, decoder_weight),
        [(narrow, bf16), ((planes, layers, rows, model), bf16)],
        decoder_weight.shape[0] * work,
    )
    columns = (Z, layers, rows // Z, model)
    (blocks,) = call(
        plane_sum_kernel,
        (lax.all_to_all(sent, PLANE, 0, 0),),
        [(columns, bf16)],
        sent.size,
        [pltpu.VMEM((rows, model), f32)],
    )
    recon, errors_home = call(
        errors_kernel,
        (lax.all_to_all(blocks, "z", 0, 0), decoder_bias, targets),
        [(targets.shape, bf16), (columns, bf16)],
        blocks.size,
    )
    errors_got = gather_plane(lax.all_to_all(errors_home, "z", 0, 0))
    (partial_grad,) = call(
        grad_kernel,
        (errors_got, decoder_weight, picked),
        [(packed, f32)],
        decoder_weight.shape[0] * work,
    )
    both, errors_got = lax.optimization_barrier((swap(partial_grad, "core"), errors_got))
    mine = (partial_grad + both).astype(bf16)
    decoder_grad, decoder_bias_grad, turned = call(
        decoder_grad_kernel,
        (activation, errors_got, gathered),
        [(decoder_weight.shape, bf16), ((layers, model), f32), ((layers, model, tokens), bf16)],
        decoder_weight.shape[0] * work,
    )
    encoder_grad, encoder_bias_grad = call(
        encoder_grad_kernel,
        (mine, swap(mine, "xl"), slots, turned),
        [((layers, model, width_here), bf16), ((layers, width_here), f32)],
        layers * work,
        [pltpu.VMEM((tokens, width_here), bf16)],
    )
    return (recon, encoder_grad, encoder_bias_grad, decoder_grad, decoder_bias_grad)


def solution(mesh):
    fine = Mesh(mesh.devices.reshape(XH, Z, Y, XL, CORE), FEAT + TOK)
    in_specs = (
        P(None, FEAT, TOK),
        P(None, FEAT, TOK),
        P(),
        P(None, TOK, FEAT),
        P(None, FEAT),
        P(None, FEAT, TOK),
        P(None, TOK),
    )
    out_specs = (
        P(None, FEAT, TOK),
        P(None, TOK, FEAT),
        P(None, FEAT),
        P(None, FEAT, TOK),
        P(None, TOK),
    )
    return jax.shard_map(body, mesh=fine, in_specs=in_specs, out_specs=out_specs, check_vma=False)
```

```python
import jax
import jax.numpy as jnp
from jax import lax
from jax.experimental import pallas as pl
from jax.experimental.pallas import tpu as pltpu
from jax.sharding import Mesh, PartitionSpec as P

FEAT = ("xh", "z", "y")
TOK = ("xl", "core")
PLANE = ("y", "xh")
XH, Z, Y, XL, CORE = 2, 16, 4, 2, 2
VMEM_BYTES = 8 << 20
bf16, f32 = jnp.bfloat16, jnp.float32


def pair_number(source, target_layer, layers):
    return sum((layers - before for before in range(source))) + target_layer - source


def swap(x, axis):
    return lax.ppermute(x, axis, [(0, 1), (1, 0)])


def copies_kernel(home_ref, out_ref, sems):
    copies = [
        pltpu.make_async_copy(home_ref, out_ref.at[z], sems.at[z])
        for z in range(out_ref.shape[0])
    ]
    for copy in copies:
        copy.start()
    for copy in copies:
        copy.wait()


def gather_z(home):
    (copies,) = call(
        copies_kernel,
        (home,),
        [((Z,) + home.shape, bf16)],
        home.size,
        [pltpu.SemaphoreType.DMA((Z,))],
        [pltpu.VMEM],
        [pl.ANY],
    )
    return lax.all_to_all(copies, "z", 0, 0)


def spread_kernel(along_z_ref, out_ref, rows_ref):
    columns, layers, rows, _ = along_z_ref.shape
    for l in range(layers):
        for z in range(columns):
            rows_ref[z * rows : (z + 1) * rows] = along_z_ref[z, l].astype(f32)
        block = rows_ref[...].astype(bf16)
        for p in range(out_ref.shape[0]):
            out_ref[p, l] = block


def gather_plane(along_z):
    columns, layers, rows, width = along_z.shape
    (block,) = call(
        spread_kernel,
        (along_z,),
        [((XH * Y, layers, columns * rows, width), bf16)],
        along_z.size,
        [pltpu.VMEM((columns * rows, width), f32)],
    )
    return lax.all_to_all(block, PLANE, 0, 0)


def plane_sum_kernel(got_ref, out_ref, rows_ref):
    columns, layers, rows, _ = out_ref.shape
    for l in range(layers):
        total = got_ref[0, l].astype(f32)
        for p in range(1, got_ref.shape[0]):
            total = total + got_ref[p, l].astype(f32)
        rows_ref[...] = total
        for z in range(columns):
            out_ref[z, l] = rows_ref[z * rows : (z + 1) * rows].astype(bf16)


def errors_kernel(got_ref, bias_ref, targets_ref, recon_ref, out_ref):
    columns, layers = got_ref.shape[:2]
    for l in range(layers):
        total = got_ref[0, l].astype(f32)
        for z in range(1, columns):
            total = total + got_ref[z, l].astype(f32)
        total = total + bias_ref[l : l + 1]
        recon_ref[l] = total.astype(bf16)
        errors = (total - targets_ref[l].astype(f32)).astype(bf16)
        for z in range(columns):
            out_ref[z, l] = errors


def rows_of(ref, layer):
    block = ref[:, layer]
    return block.reshape(block.shape[0] * block.shape[1], block.shape[2])


def mask_kernel(winners_ref, slot_ref, pick_ref, marks_ref):
    layers, picks, tokens = winners_ref.shape
    features = slot_ref.shape[2]
    half, near = features // 2, tokens // 2
    for l in range(layers):
        for h in range(0, features, half):
            ids = h + lax.broadcasted_iota(jnp.int32, (half, tokens), 0)
            marks = jnp.zeros((half, tokens), f32)
            for k in range(picks):
                marks = jnp.where(winners_ref[l, k : k + 1, :] == ids, float(k + 1), marks)
            marks_ref[h : h + half] = marks
        slot_ref[l] = marks_ref[...].T.astype(jnp.int32)
        here = jnp.clip(winners_ref[l], 0, features - 1).astype(f32)
        marks_ref[:picks, :near] = here[:, :near]
        marks_ref[picks : 2 * picks, :near] = here[:, near:]
        pick_ref[l] = marks_ref[:, :near].T.astype(jnp.int32)


def take(values, places):
    return jnp.take_along_axis(values, places, axis=1, mode="promise_in_bounds")


def pack(values, pick):
    near, lanes = pick.shape
    first = lax.broadcasted_iota(jnp.int32, (near, lanes), 1) < lanes // 2
    return jnp.where(first, take(values[:near], pick), take(values[near:], pick))


def unpack(packed, slot_ref, layer):
    near, lanes = packed.shape
    for part in range(2):
        rows = slice(part * near, (part + 1) * near)
        slot = slot_ref[layer, rows]
        place = jnp.maximum(slot - 1, 0) + part * (lanes // 2)
        yield rows, slot > 0, take(packed, place)


def encode_kernel(x_ref, weight_ref, pick_ref, out_ref):
    for l in range(out_ref.shape[0]):
        pre_acts = jnp.dot(rows_of(x_ref, l), weight_ref[l], preferred_element_type=f32)
        out_ref[l] = pack(pre_acts, pick_ref[l])


def decode_kernel(mine_ref, theirs_ref, bias_ref, slot_ref, weight_ref, act_ref, out_ref):
    layers = act_ref.shape[0]
    for l in range(layers):
        packed = mine_ref[l].astype(f32) + theirs_ref[l].astype(f32)
        for rows, chosen, values in unpack(packed, slot_ref, l):
            pre_acts = values + bias_ref[l : l + 1]
            act_ref[l, rows] = jnp.where(chosen, pre_acts, 0.0).astype(bf16)
    for u in range(layers):
        totals = None
        for s in range(u + 1):
            product = jnp.dot(
                act_ref[s], weight_ref[pair_number(s, u, layers)], preferred_element_type=f32
            )
            totals = product if totals is None else totals + product
        out_ref[:, u] = totals.astype(bf16).reshape(
            out_ref.shape[0], out_ref.shape[2], out_ref.shape[3]
        )


def grad_kernel(errors_ref, weight_ref, pick_ref, out_ref):
    layers = out_ref.shape[0]
    for s in range(layers):
        grad_act = None
        for u in range(s, layers):
            product = lax.dot_general(
                rows_of(errors_ref, u),
                weight_ref[pair_number(s, u, layers)],
                (((1,), (1,)), ((), ())),
                preferred_element_type=f32,
            )
            grad_act = product if grad_act is None else grad_act + product
        out_ref[s] = pack(grad_act, pick_ref[s])


def decoder_grad_kernel(act_ref, errors_ref, x_ref, out_ref, bias_ref, turned_ref):
    layers = act_ref.shape[0]
    for l in range(layers):
        turned_ref[l] = rows_of(x_ref, l).T
    for u in range(layers):
        errors = rows_of(errors_ref, u)
        bias_ref[u : u + 1] = jnp.sum(errors.astype(f32), axis=0, keepdims=True)
        for s in range(u + 1):
            out_ref[pair_number(s, u, layers)] = lax.dot_general(
                act_ref[s], errors, (((0,), (0,)), ((), ())), preferred_element_type=f32
            ).astype(bf16)


def encoder_grad_kernel(
    mine_ref, theirs_ref, slot_ref, turned_ref, out_ref, bias_ref, grad_ref, held_ref, sems
):
    copies = []
    for l in range(out_ref.shape[0]):
        packed = mine_ref[l].astype(f32) + theirs_ref[l].astype(f32)
        for rows, chosen, values in unpack(packed, slot_ref, l):
            grad_ref[rows] = jnp.where(chosen, values, 0.0).astype(bf16)
        grad_pre = grad_ref[...]
        held_ref[l] = jnp.dot(
            turned_ref[l], grad_pre, preferred_element_type=f32
        ).astype(bf16)
        copies.append(pltpu.make_async_copy(held_ref.at[l], out_ref.at[l], sems.at[l]))
        copies[l].start()
        bias_ref[l : l + 1] = jnp.sum(grad_pre.astype(f32), axis=0, keepdims=True)
    for copy in copies:
        copy.wait()


def call(kernel, args, outs, flops, scratch=(), spaces_in=None, spaces_out=None):
    size = sum(a.size * a.dtype.itemsize for a in args)
    return pl.pallas_call(
        kernel,
        out_shape=[jax.ShapeDtypeStruct(shape, kind) for shape, kind in outs],
        in_specs=[
            pl.BlockSpec(memory_space=space) for space in spaces_in or [pltpu.VMEM] * len(args)
        ],
        out_specs=[
            pl.BlockSpec(memory_space=space) for space in spaces_out or [pltpu.VMEM] * len(outs)
        ],
        scratch_shapes=list(scratch),
        compiler_params=pltpu.CompilerParams(vmem_limit_bytes=VMEM_BYTES),
        cost_estimate=pl.CostEstimate(flops=flops, bytes_accessed=2 * size, transcendentals=0),
    )(*args)


def body(
    layer_inputs, targets, winners, encoder_weight, encoder_bias, decoder_weight, decoder_bias
):
    layers = layer_inputs.shape[0]
    width_here = encoder_weight.shape[2]
    picks = winners.shape[2]
    tokens = winners.shape[1]
    model = encoder_weight.shape[1]

    along_z = gather_z(layer_inputs)

    order = winners.reshape(layers, XH, Z, Y, 2, picks).transpose(0, 5, 3, 1, 2, 4)
    order = order.reshape(layers, picks, tokens) - lax.axis_index(FEAT) * width_here
    slots, picked = call(
        mask_kernel,
        (order,),
        [
            ((layers, tokens, width_here), jnp.int32),
            ((layers, tokens // 2, 2 * picks), jnp.int32),
        ],
        layers * picks * tokens * width_here,
        [pltpu.VMEM((width_here, tokens), f32)],
    )
    along_z, slots, picked = lax.optimization_barrier((along_z, slots, picked))
    gathered = gather_plane(along_z)

    planes, rows = XH * Y, tokens // (XH * Y)
    narrow = (layers, tokens, width_here)
    packed = (layers, tokens // 2, 2 * picks)
    work = 2 * tokens * width_here * model
    (partial_pre,) = call(
        encode_kernel, (gathered, encoder_weight, picked), [(packed, f32)], layers * work
    )
    mine = (partial_pre + swap(partial_pre, "core")).astype(bf16)
    activation, sent = call(
        decode_kernel,
        (mine, swap(mine, "xl"), encoder_bias, slots, decoder_weight),
        [(narrow, bf16), ((planes, layers, rows, model), bf16)],
        decoder_weight.shape[0] * work,
    )
    columns = (Z, layers, rows // Z, model)
    (blocks,) = call(
        plane_sum_kernel,
        (lax.all_to_all(sent, PLANE, 0, 0),),
        [(columns, bf16)],
        sent.size,
        [pltpu.VMEM((rows, model), f32)],
    )
    recon, errors_home = call(
        errors_kernel,
        (lax.all_to_all(blocks, "z", 0, 0), decoder_bias, targets),
        [(targets.shape, bf16), (columns, bf16)],
        blocks.size,
    )
    errors_got = gather_plane(lax.all_to_all(errors_home, "z", 0, 0))
    (partial_grad,) = call(
        grad_kernel,
        (errors_got, decoder_weight, picked),
        [(packed, f32)],
        decoder_weight.shape[0] * work,
    )
    both, errors_got = lax.optimization_barrier((swap(partial_grad, "core"), errors_got))
    mine = (partial_grad + both).astype(bf16)
    decoder_grad, decoder_bias_grad, turned = call(
        decoder_grad_kernel,
        (activation, errors_got, gathered),
        [(decoder_weight.shape, bf16), ((layers, model), f32), ((layers, model, tokens), bf16)],
        decoder_weight.shape[0] * work,
    )
    encoder_grad, encoder_bias_grad = call(
        encoder_grad_kernel,
        (mine, swap(mine, "xl"), slots, turned),
        [((layers, model, width_here), bf16), ((layers, width_here), f32)],
        layers * work,
        [
            pltpu.VMEM((tokens, width_here), bf16),
            pltpu.VMEM((layers, model, width_here), bf16),
            pltpu.SemaphoreType.DMA((layers,)),
        ],
        None,
        [pl.ANY, pltpu.VMEM],
    )
    return (recon, encoder_grad, encoder_bias_grad, decoder_grad, decoder_bias_grad)


def solution(mesh):
    fine = Mesh(mesh.devices.reshape(XH, Z, Y, XL, CORE), FEAT + TOK)
    in_specs = (
        P(None, FEAT, TOK),
        P(None, FEAT, TOK),
        P(),
        P(None, TOK, FEAT),
        P(None, FEAT),
        P(None, FEAT, TOK),
        P(None, TOK),
    )
    out_specs = (
        P(None, FEAT, TOK),
        P(None, TOK, FEAT),
        P(None, FEAT),
        P(None, FEAT, TOK),
        P(None, TOK),
    )
    return jax.shard_map(body, mesh=fine, in_specs=in_specs, out_specs=out_specs, check_vma=False)
```

```python
import jax
import jax.numpy as jnp
from jax import lax
from jax.experimental import pallas as pl
from jax.experimental.pallas import tpu as pltpu
from jax.sharding import Mesh, PartitionSpec as P

FEAT = ("xh", "zh", "zl", "y")
COLUMN = ("zl", "zh")
TOK = ("xl", "core")
PLANE = ("y", "xh")
XH, ZH, ZL, Y, XL, CORE = 2, 4, 4, 4, 2, 2
Z = ZH * ZL
VMEM_BYTES = 8 << 20
bf16, f32 = jnp.bfloat16, jnp.float32


def pair_number(source, target_layer, layers):
    return sum((layers - before for before in range(source))) + target_layer - source


def swap(x, axis):
    return lax.ppermute(x, axis, [(0, 1), (1, 0)])


def copies_kernel(home_ref, out_ref):
    for z in range(out_ref.shape[0]):
        out_ref[z] = home_ref[...]


def gather_z(home):
    (copies,) = call(copies_kernel, (home,), [((Z,) + home.shape, bf16)], home.size)
    return lax.all_to_all(copies, COLUMN, 0, 0)


def spread_kernel(along_z_ref, out_ref, rows_ref):
    columns, layers, rows, _ = along_z_ref.shape
    for l in range(layers):
        for z in range(columns):
            rows_ref[z * rows : (z + 1) * rows] = along_z_ref[z, l].astype(f32)
        block = rows_ref[...].astype(bf16)
        for p in range(out_ref.shape[0]):
            out_ref[p, l] = block


def gather_plane(along_z):
    columns, layers, rows, width = along_z.shape
    (block,) = call(
        spread_kernel,
        (along_z,),
        [((XH * Y, layers, columns * rows, width), bf16)],
        along_z.size,
        [pltpu.VMEM((columns * rows, width), f32)],
    )
    return lax.all_to_all(block, PLANE, 0, 0)


def plane_sum_kernel(got_ref, out_ref, rows_ref):
    columns, layers, rows, _ = out_ref.shape
    for l in range(layers):
        total = got_ref[0, l].astype(f32)
        for p in range(1, got_ref.shape[0]):
            total = total + got_ref[p, l].astype(f32)
        rows_ref[...] = total
        for z in range(columns):
            out_ref[z, l] = rows_ref[z * rows : (z + 1) * rows].astype(bf16)


def errors_kernel(got_ref, bias_ref, targets_ref, recon_ref, out_ref):
    columns, layers = got_ref.shape[:2]
    for l in range(layers):
        total = got_ref[0, l].astype(f32)
        for z in range(1, columns):
            total = total + got_ref[z, l].astype(f32)
        total = total + bias_ref[l : l + 1]
        recon_ref[l] = total.astype(bf16)
        errors = (total - targets_ref[l].astype(f32)).astype(bf16)
        for z in range(columns):
            out_ref[z, l] = errors


def rows_of(ref, layer):
    block = ref[:, layer]
    return block.reshape(block.shape[0] * block.shape[1], block.shape[2])


def mask_kernel(winners_ref, slot_ref, pick_ref, marks_ref):
    layers, picks, tokens = winners_ref.shape
    features = slot_ref.shape[2]
    half, near = features // 2, tokens // 2
    for l in range(layers):
        for h in range(0, features, half):
            ids = h + lax.broadcasted_iota(jnp.int32, (half, tokens), 0)
            marks = jnp.zeros((half, tokens), f32)
            for k in range(picks):
                marks = jnp.where(winners_ref[l, k : k + 1, :] == ids, float(k + 1), marks)
            marks_ref[h : h + half] = marks
        slot_ref[l] = marks_ref[...].T.astype(jnp.int32)
        here = jnp.clip(winners_ref[l], 0, features - 1).astype(f32)
        marks_ref[:picks, :near] = here[:, :near]
        marks_ref[picks : 2 * picks, :near] = here[:, near:]
        pick_ref[l] = marks_ref[:, :near].T.astype(jnp.int32)


def take(values, places):
    return jnp.take_along_axis(values, places, axis=1, mode="promise_in_bounds")


def pack(values, pick):
    near, lanes = pick.shape
    first = lax.broadcasted_iota(jnp.int32, (near, lanes), 1) < lanes // 2
    return jnp.where(first, take(values[:near], pick), take(values[near:], pick))


def unpack(packed, slot_ref, layer):
    near, lanes = packed.shape
    for part in range(2):
        rows = slice(part * near, (part + 1) * near)
        slot = slot_ref[layer, rows]
        place = jnp.maximum(slot - 1, 0) + part * (lanes // 2)
        yield rows, slot > 0, take(packed, place)


def encode_kernel(x_ref, weight_ref, pick_ref, out_ref):
    for l in range(out_ref.shape[0]):
        pre_acts = jnp.dot(rows_of(x_ref, l), weight_ref[l], preferred_element_type=f32)
        out_ref[l] = pack(pre_acts, pick_ref[l])


def decode_kernel(mine_ref, theirs_ref, bias_ref, slot_ref, weight_ref, act_ref, out_ref):
    layers = act_ref.shape[0]
    for l in range(layers):
        packed = mine_ref[l].astype(f32) + theirs_ref[l].astype(f32)
        for rows, chosen, values in unpack(packed, slot_ref, l):
            pre_acts = values + bias_ref[l : l + 1]
            act_ref[l, rows] = jnp.where(chosen, pre_acts, 0.0).astype(bf16)
    for u in range(layers):
        totals = None
        for s in range(u + 1):
            product = jnp.dot(
                act_ref[s], weight_ref[pair_number(s, u, layers)], preferred_element_type=f32
            )
            totals = product if totals is None else totals + product
        out_ref[:, u] = totals.astype(bf16).reshape(
            out_ref.shape[0], out_ref.shape[2], out_ref.shape[3]
        )


def grad_kernel(errors_ref, weight_ref, pick_ref, out_ref):
    layers = out_ref.shape[0]
    for s in range(layers):
        grad_act = None
        for u in range(s, layers):
            product = lax.dot_general(
                rows_of(errors_ref, u),
                weight_ref[pair_number(s, u, layers)],
                (((1,), (1,)), ((), ())),
                preferred_element_type=f32,
            )
            grad_act = product if grad_act is None else grad_act + product
        out_ref[s] = pack(grad_act, pick_ref[s])


def decoder_grad_kernel(act_ref, errors_ref, x_ref, out_ref, bias_ref, turned_ref):
    layers = act_ref.shape[0]
    for l in range(layers):
        turned_ref[l] = rows_of(x_ref, l).T
    for u in range(layers):
        errors = rows_of(errors_ref, u)
        bias_ref[u : u + 1] = jnp.sum(errors.astype(f32), axis=0, keepdims=True)
        for s in range(u + 1):
            out_ref[pair_number(s, u, layers)] = lax.dot_general(
                act_ref[s], errors, (((0,), (0,)), ((), ())), preferred_element_type=f32
            ).astype(bf16)


def encoder_grad_kernel(mine_ref, theirs_ref, slot_ref, turned_ref, out_ref, bias_ref, grad_ref):
    for l in range(out_ref.shape[0]):
        packed = mine_ref[l].astype(f32) + theirs_ref[l].astype(f32)
        for rows, chosen, values in unpack(packed, slot_ref, l):
            grad_ref[rows] = jnp.where(chosen, values, 0.0).astype(bf16)
        grad_pre = grad_ref[...]
        bias_ref[l : l + 1] = jnp.sum(grad_pre.astype(f32), axis=0, keepdims=True)
        out_ref[l] = jnp.dot(
            turned_ref[l], grad_pre, preferred_element_type=f32
        ).astype(bf16)


def call(kernel, args, outs, flops, scratch=()):
    size = sum(a.size * a.dtype.itemsize for a in args)
    return pl.pallas_call(
        kernel,
        out_shape=[jax.ShapeDtypeStruct(shape, kind) for shape, kind in outs],
        in_specs=[pl.BlockSpec(memory_space=pltpu.VMEM) for _ in args],
        out_specs=[pl.BlockSpec(memory_space=pltpu.VMEM) for _ in outs],
        scratch_shapes=list(scratch),
        compiler_params=pltpu.CompilerParams(vmem_limit_bytes=VMEM_BYTES),
        cost_estimate=pl.CostEstimate(flops=flops, bytes_accessed=2 * size, transcendentals=0),
    )(*args)


def body(
    layer_inputs, targets, winners, encoder_weight, encoder_bias, decoder_weight, decoder_bias
):
    layers = layer_inputs.shape[0]
    width_here = encoder_weight.shape[2]
    picks = winners.shape[2]
    tokens = winners.shape[1]
    model = encoder_weight.shape[1]

    along_z = gather_z(layer_inputs)

    order = winners.reshape(layers, XH, ZH, ZL, Y, 2, picks).transpose(0, 6, 4, 1, 3, 2, 5)
    order = order.reshape(layers, picks, tokens) - lax.axis_index(FEAT) * width_here
    slots, picked = call(
        mask_kernel,
        (order,),
        [
            ((layers, tokens, width_here), jnp.int32),
            ((layers, tokens // 2, 2 * picks), jnp.int32),
        ],
        layers * picks * tokens * width_here,
        [pltpu.VMEM((width_here, tokens), f32)],
    )
    along_z, slots, picked = lax.optimization_barrier((along_z, slots, picked))
    gathered = gather_plane(along_z)

    planes, rows = XH * Y, tokens // (XH * Y)
    narrow = (layers, tokens, width_here)
    packed = (layers, tokens // 2, 2 * picks)
    work = 2 * tokens * width_here * model
    (partial_pre,) = call(
        encode_kernel, (gathered, encoder_weight, picked), [(packed, f32)], layers * work
    )
    mine = (partial_pre + swap(partial_pre, "core")).astype(bf16)
    activation, sent = call(
        decode_kernel,
        (mine, swap(mine, "xl"), encoder_bias, slots, decoder_weight),
        [(narrow, bf16), ((planes, layers, rows, model), bf16)],
        decoder_weight.shape[0] * work,
    )
    columns = (Z, layers, rows // Z, model)
    (blocks,) = call(
        plane_sum_kernel,
        (lax.all_to_all(sent, PLANE, 0, 0),),
        [(columns, bf16)],
        sent.size,
        [pltpu.VMEM((rows, model), f32)],
    )
    recon, errors_home = call(
        errors_kernel,
        (lax.all_to_all(blocks, COLUMN, 0, 0), decoder_bias, targets),
        [(targets.shape, bf16), (columns, bf16)],
        blocks.size,
    )
    errors_got = gather_plane(lax.all_to_all(errors_home, COLUMN, 0, 0))
    (partial_grad,) = call(
        grad_kernel,
        (errors_got, decoder_weight, picked),
        [(packed, f32)],
        decoder_weight.shape[0] * work,
    )
    both, errors_got = lax.optimization_barrier((swap(partial_grad, "core"), errors_got))
    mine = (partial_grad + both).astype(bf16)
    decoder_grad, decoder_bias_grad, turned = call(
        decoder_grad_kernel,
        (activation, errors_got, gathered),
        [(decoder_weight.shape, bf16), ((layers, model), f32), ((layers, model, tokens), bf16)],
        decoder_weight.shape[0] * work,
    )
    encoder_grad, encoder_bias_grad = call(
        encoder_grad_kernel,
        (mine, swap(mine, "xl"), slots, turned),
        [((layers, model, width_here), bf16), ((layers, width_here), f32)],
        layers * work,
        [pltpu.VMEM((tokens, width_here), bf16)],
    )
    return (recon, encoder_grad, encoder_bias_grad, decoder_grad, decoder_bias_grad)


def solution(mesh):
    fine = Mesh(mesh.devices.reshape(XH, ZH, ZL, Y, XL, CORE), FEAT + TOK)
    in_specs = (
        P(None, FEAT, TOK),
        P(None, FEAT, TOK),
        P(),
        P(None, TOK, FEAT),
        P(None, FEAT),
        P(None, FEAT, TOK),
        P(None, TOK),
    )
    out_specs = (
        P(None, FEAT, TOK),
        P(None, TOK, FEAT),
        P(None, FEAT),
        P(None, FEAT, TOK),
        P(None, TOK),
    )
    return jax.shard_map(body, mesh=fine, in_specs=in_specs, out_specs=out_specs, check_vma=False)
```
